32 devices in a mesh: groups: 2 (over y), replica: 4 (over z), tensor: 4 (over x, core).
Axes of the slice: x: 2, y: 2, z: 4, core: 2. Of those that a mesh axis runs over, the one named last changes fastest.
Arguments:
- normed_hidden_rows: bfloat16 [1024, 8192], P(('groups', 'replica')), parts along dimension 0, may hold values from -6 to 6
- queries: bfloat16 [1024, 64, 128], P(('groups', 'replica'), 'tensor'), parts along dimension 0, may hold values from -8 to 8
- incoming_key: bfloat16 [1024, 8, 128], P(('groups', 'replica'), 'tensor'), parts along dimension 0, may hold values from -5 to 5
- stored_key_cache: bfloat16 [1024, 64, 8, 128], P(('groups', 'replica'), None, 'tensor'), parts along dimension 0, may hold values from -5 to 5
- stored_value_cache: bfloat16 [1024, 64, 8, 128], P(('groups', 'replica'), None, 'tensor'), parts along dimension 0, may hold values from -6 to 6
- value_weight: bfloat16 [8192, 1024], P(None, 'tensor'), may hold values from -0.0625 to 0.0625
- adapter_down_weight: bfloat16 [16, 64, 8192], P('replica', None, 'tensor'), may hold values from -0.0625 to 0.0625
- adapter_up_weight: bfloat16 [16, 64, 1024], P('replica', None, 'tensor'), may hold values from -0.75 to 0.75
- token_adapter_index: int32 [1024], P(('groups', 'replica')), parts along dimension 0, may hold values from 0 to 15, as said below
- adapter_holder_replica: int32 [32], P('groups'), parts along dimension 0, may hold values from 0 to 3, as said below
- refill: int32 [1024], P(('groups', 'replica')), parts along dimension 0, may hold values 0 or 1
Outputs:
- incoming_value: bfloat16 [1024, 1024], P(('groups', 'replica'), 'tensor'), parts along dimension 0
- attended: bfloat16 [1024, 8192], P(('groups', 'replica'), 'tensor'), parts along dimension 0
The draws below stay inside these ranges and needn't reach their ends.
There are 2 independent parts, one for each index of `groups`. The reference program is written for one: setup_inputs(seed, part) draws one part's arguments, and reference() takes and returns one part's arrays. A program takes and returns all parts, laid end to end along the dimension named above; an argument that names none is the same for every part. Nothing has to cross between parts.
Inputs may be any that keep to these rules, and one draw needn't show every extreme that they name: `adapter_holder_replica`: every replica index owns exactly 4 adapters. `token_adapter_index`: among the 128 tokens of one replica (tokens 128*r to 128*r + 127), at most 32 use adapters owned by one replica; some replica owns the adapters of exactly 32 tokens of every replica.
All inputs are finite; a program needn't handle non-finite values. No bound on the sum of `refill` on one device may be relied on, other than what follows from the above.
Results may differ from the reference program's by a relative error of at most 0.0055.
Values may be sent and summed in bfloat16 or wider, within the bound.
No kernel may reach another device: no remote copies, remote signals or barrier semaphores. Data moves between devices by JAX's collectives and lax.ppermute only.
A program may use at most 64 MiB of HBM per device.

```python
import jax
import jax.numpy as jnp
from jax import lax

MODEL_WIDTH = 8192
H = 64
KEY_VALUE_HEADS = 8
HEAD_WIDTH = 128
ADAPTER_RANK = 64
ROWS = 128
CACHE = 64
ADP_DEV = 4
CAP = 32
TOKENS = 512
ADAPTER_TOTAL = 16
N_REPLICA = 4


def routing_tables(key):
    shuffle = jax.random.permutation(jax.random.fold_in(key, 11), ADAPTER_TOTAL).astype(jnp.int32)
    common_owner = jax.random.randint(jax.random.fold_in(key, 12), (), 0, N_REPLICA).astype(jnp.int32)

    def replica_rows(row_key):
        key_a, key_b, key_c = jax.random.split(row_key, 3)
        spare_slots = CAP + jax.random.permutation(key_a, N_REPLICA * CAP - CAP).astype(jnp.int32)
        slot_list = jnp.concatenate([jnp.arange(CAP, dtype=jnp.int32), spare_slots])[:ROWS]
        groups = slot_list // CAP
        owners = (common_owner + groups) % N_REPLICA
        owners = owners[jax.random.permutation(key_b, ROWS)]
        picked = jax.random.randint(key_c, (ROWS,), 0, ADP_DEV).astype(jnp.int32)
        return owners * ADP_DEV + picked
    row_keys = jax.random.split(jax.random.fold_in(key, 13), N_REPLICA)
    store_index = jax.vmap(replica_rows)(row_keys).reshape(-1)
    inverse = jnp.argsort(shuffle).astype(jnp.int32)
    return ((shuffle // ADP_DEV).astype(jnp.int32), inverse[store_index].astype(jnp.int32))


def shared_keys(key):
    return jnp.clip(jax.random.normal(jax.random.fold_in(key, 100), (TOKENS, KEY_VALUE_HEADS, HEAD_WIDTH), jnp.float32), -5.0, 5.0)


def draw_adapter_holder_replica(key, part):
    owners, chosen = routing_tables(key)
    return owners


def draw_token_adapter_index(key, part):
    owners, chosen = routing_tables(key)
    return chosen


def draw_incoming_key(key, part):
    return shared_keys(key).astype(jnp.bfloat16)


def draw_queries(key, part):
    fresh = shared_keys(key)
    key = jax.random.fold_in(key, 5)
    group_size = H // KEY_VALUE_HEADS
    noise_part = jnp.clip(jax.random.normal(key, (TOKENS, H, HEAD_WIDTH), jnp.float32), -5.0, 5.0)
    result = 0.4 * jnp.repeat(fresh, group_size, axis=1) + noise_part
    return result.astype(jnp.bfloat16)


def draw_stored_key_cache(key, part):
    key = jax.random.fold_in(key, 7)
    result = jnp.clip(jax.random.normal(key, (TOKENS, CACHE, KEY_VALUE_HEADS, HEAD_WIDTH), jnp.float32), -5.0, 5.0)
    return result.astype(jnp.bfloat16)


def with_ends(values, stream_key, smallest, largest):
    longest = values.shape.index(max(values.shape))
    spots = []
    for shift in (0, 1):
        where = [jax.random.randint(jax.random.fold_in(stream_key, axis), (), 0, length) for axis, length in enumerate(values.shape)]
        where[longest] = (where[longest] + shift) % values.shape[longest]
        spots.append(tuple(where))
    return values.at[spots[0]].set(smallest).at[spots[1]].set(largest)


def levels(stream_key, dims, pieces, least, top_value):
    gain, own = 1.0, jax.random.fold_in(stream_key, 6)
    for axis_at, parts in pieces:
        steps = jnp.exp(jax.random.uniform(jax.random.fold_in(own, axis_at), (parts,), jnp.float32, least / len(pieces), top_value / len(pieces)))
        gain = gain * jnp.repeat(steps, dims[axis_at] // parts).reshape([-1 if axis == axis_at else 1 for axis in range(len(dims))])
    return gain


def gaussian(rng, dims, spread, limit, pieces=(), held_as=jnp.bfloat16):
    values = jax.random.normal(rng, dims, jnp.float32) * spread
    if len(pieces) > 0:
        values = levels(rng, dims, pieces, -0.22, 0.18) * values
    return jnp.clip(values, min=-limit, max=limit).astype(held_as)


def setup_inputs(seed: int = 0, part: int = 0) -> dict:
    splits = jax.random.split(jax.random.key(seed), 12)
    part_keys = jax.random.split(jax.random.fold_in(splits[11], part), 12)
    return {
        "normed_hidden_rows": gaussian(part_keys[0], (TOKENS, MODEL_WIDTH), 1.0, 6.0, ((0, 4),)),
        "queries": draw_queries(jax.random.fold_in(jax.random.fold_in(splits[11], part), 71), part),
        "incoming_key": draw_incoming_key(jax.random.fold_in(jax.random.fold_in(splits[11], part), 71), part),
        "stored_key_cache": draw_stored_key_cache(jax.random.fold_in(jax.random.fold_in(splits[11], part), 71), part),
        "stored_value_cache": gaussian(part_keys[4], (TOKENS, CACHE, KEY_VALUE_HEADS, HEAD_WIDTH), 1.0, 6.0, ((0, 4), (2, 4))),
        "value_weight": gaussian(splits[5], (MODEL_WIDTH, KEY_VALUE_HEADS * HEAD_WIDTH), MODEL_WIDTH ** -0.5, 0.0625, ((1, 4),)),
        "adapter_down_weight": gaussian(splits[6], (ADAPTER_TOTAL, ADAPTER_RANK, MODEL_WIDTH), MODEL_WIDTH ** -0.5, 0.0625, ((0, 4), (2, 4))),
        "adapter_up_weight": gaussian(splits[7], (ADAPTER_TOTAL, ADAPTER_RANK, KEY_VALUE_HEADS * HEAD_WIDTH), ADAPTER_RANK ** -0.5, 0.75, ((0, 4), (2, 4))),
        "token_adapter_index": draw_token_adapter_index(jax.random.fold_in(jax.random.fold_in(splits[11], part), 71), part),
        "adapter_holder_replica": draw_adapter_holder_replica(jax.random.fold_in(jax.random.fold_in(splits[11], part), 71), part),
        "refill": with_ends((jax.random.randint(part_keys[10], (TOKENS,), 0, 4) < 1).astype(jnp.int32), jax.random.fold_in(part_keys[10], 1), 0, 1),
    }


adapter_output_scale = 0.5
mask_value = -1e30


def adapter_store_slots(adapter_holder_replica, per_owner):
    count_all = adapter_holder_replica.shape[0]
    row_order = jnp.arange(count_all, dtype=jnp.int32)
    earlier = (adapter_holder_replica[:, None] == adapter_holder_replica[None, :]) & (row_order[None, :] < row_order[:, None])
    return adapter_holder_replica * per_owner + jnp.sum(earlier.astype(jnp.int32), axis=1)


def reference(normed_hidden_rows, queries, incoming_key, stored_key_cache, stored_value_cache, value_weight, adapter_down_weight, adapter_up_weight, token_adapter_index, adapter_holder_replica, refill):
    slot_table = adapter_store_slots(adapter_holder_replica, ADP_DEV)
    token_row_slot = slot_table[token_adapter_index]

    def adapter_table_row(row_item):
        x_row, slot_token_row = row_item
        down_weight_rows = adapter_down_weight[slot_token_row]
        up_weight_rows = adapter_up_weight[slot_token_row]
        shrink_output = jnp.dot(down_weight_rows, x_row, preferred_element_type=jnp.float32).astype(jnp.bfloat16)
        return jnp.dot(shrink_output, up_weight_rows, preferred_element_type=jnp.float32)

    adapter_value_term = lax.map(adapter_table_row, (normed_hidden_rows, token_row_slot))
    base_value_output = jnp.dot(normed_hidden_rows, value_weight, preferred_element_type=jnp.float32)
    incoming_value = (base_value_output + adapter_output_scale * adapter_value_term).astype(jnp.bfloat16)

    group_size = H // KEY_VALUE_HEADS
    score_scale = HEAD_WIDTH ** -0.5

    def attend_row(row_item):
        query_row, keys_row, values_row, fresh_key, fresh_value, refill_row = row_item
        query_all = query_row.astype(jnp.float32).reshape(KEY_VALUE_HEADS, group_size, HEAD_WIDTH)
        scores = jnp.einsum("kgd,ckd->kgc", query_all, keys_row.astype(jnp.float32)) * score_scale
        scores = jnp.where(refill_row == 1, mask_value, scores)
        fresh_score = jnp.einsum("kgd,kd->kg", query_all, fresh_key.astype(jnp.float32)) * score_scale
        row_top = jnp.maximum(jnp.max(scores, axis=-1), fresh_score)
        cache_exp = jnp.exp(scores - row_top[:, :, None])
        fresh_exp = jnp.exp(fresh_score - row_top)
        denominator = jnp.sum(cache_exp, axis=-1) + fresh_exp
        cache_weight = (cache_exp / denominator[:, :, None]).astype(jnp.bfloat16)
        fresh_weight = (fresh_exp / denominator).astype(jnp.bfloat16)
        output = jnp.einsum("kgc,ckd->kgd", cache_weight.astype(jnp.float32), values_row.astype(jnp.float32))
        value_heads = fresh_value.reshape(KEY_VALUE_HEADS, HEAD_WIDTH).astype(jnp.float32)
        output = output + fresh_weight.astype(jnp.float32)[:, :, None] * value_heads[:, None, :]
        return output.reshape(H * HEAD_WIDTH).astype(jnp.bfloat16)

    attended = lax.map(attend_row, (queries, stored_key_cache, stored_value_cache, incoming_key, incoming_value, refill))
    return incoming_value, attended
```

```python
import functools

import jax
import jax.numpy as jnp
from jax import lax
from jax.experimental import pallas as pl
from jax.experimental.pallas import tpu as pltpu
from jax.sharding import PartitionSpec as P

adapter_output_scale = 0.5
mask_value = -1e30
LANES = 128
VMEM = pl.BlockSpec(memory_space=pltpu.VMEM)
ANY = pl.BlockSpec(memory_space=pl.ANY)
F32 = jnp.float32
BF16 = jnp.bfloat16


def iota(shape, dimension):
    return lax.broadcasted_iota(jnp.int32, shape, dimension)


def to_column(row):
    size = row.shape[1]
    eye = iota((size, size), 0) == iota((size, size), 1)
    return jnp.sum(jnp.where(eye, row, 0.0), axis=1, keepdims=True)


def partner_pairs(replicas, step):
    if replicas & (replicas - 1) == 0:
        return [(r, r ^ step) for r in range(replicas)]
    return [(r, (r + step) % replicas) for r in range(replicas)]


def return_pairs(replicas, step):
    return [(b, a) for a, b in partner_pairs(replicas, step)]


def route_kernel(replicas, block, tokens_ref, holder_ref, x_ref, *refs):
    messages, order_ref, x_buf, sems = refs[:replicas], refs[replicas], refs[-2], refs[-1]
    rows, width = x_buf.shape
    pieces = sems.shape[0]
    piece = width // pieces
    first = lax.axis_index("tensor") * width
    copies = [
        pltpu.make_async_copy(
            x_ref.at[:, pl.ds(pl.multiple_of(first + i * piece, LANES), piece)],
            x_buf.at[:, pl.ds(i * piece, piece)],
            sems.at[i],
        )
        for i in range(pieces)
    ]
    for copy in copies:
        copy.start()
    me = lax.axis_index("replica")
    adapters = holder_ref.shape[1]
    holder_row = holder_ref[...].astype(F32)
    holder_col = to_column(holder_row)
    earlier = (holder_col == holder_row) & (
        iota((adapters, adapters), 1) < iota((adapters, adapters), 0)
    )
    rank_col = jnp.sum(jnp.where(earlier, 1.0, 0.0), axis=1, keepdims=True)
    uses = tokens_ref[...] == iota((adapters, rows), 0)
    owner_row = jnp.sum(jnp.where(uses, holder_col, 0.0), axis=0, keepdims=True)
    local_row = jnp.sum(jnp.where(uses, rank_col, 0.0), axis=0, keepdims=True)
    owner_col = to_column(owner_row)
    before = (owner_col == owner_row) & (iota((rows, rows), 0) < iota((rows, rows), 1))
    place_row = jnp.sum(jnp.where(before, 1.0, 0.0), axis=0, keepdims=True)
    owner_int = owner_row.astype(jnp.int32)
    if replicas & (replicas - 1) == 0:
        step_row = owner_int ^ me
    else:
        step_row = owner_int - me
        step_row = jnp.where(step_row < 0, step_row + replicas, step_row)
    target_row = step_row * block + place_row.astype(jnp.int32)
    target_col = to_column(target_row.astype(F32)).astype(jnp.int32)
    local_col = to_column(local_row)
    slots = replicas * block
    select = (target_row == iota((slots, rows), 0)).astype(F32).astype(BF16)
    restore = (target_col == iota((rows, slots), 1)).astype(F32)
    order_ref[...] = restore.astype(BF16)
    local_by_slot = jnp.sum(restore * local_col, axis=0, keepdims=True)
    for k in range(replicas):
        lane = k * block // LANES * LANES
        tail = jnp.broadcast_to(local_by_slot[:, lane : lane + LANES], (16, LANES))
        messages[k][width // LANES * block :, :] = tail.astype(BF16)
    for i, copy in enumerate(copies):
        copy.wait()
        moved = jnp.dot(
            select, x_buf[:, i * piece : (i + 1) * piece], preferred_element_type=F32
        ).astype(BF16)
        for k in range(replicas):
            for j in range(piece // LANES):
                at = (i * (piece // LANES) + j) * block
                messages[k][at : at + block, :] = moved[
                    k * block : (k + 1) * block, j * LANES : (j + 1) * LANES
                ]


def shrink_kernel(replicas, block, *refs):
    messages, down_ref, partial_ref, local_ref = refs[:replicas], *refs[replicas:]
    count, rank, width = down_ref.shape
    slots = replicas * block
    chunks = width // LANES
    gathered = [
        jnp.concatenate(
            [messages[k][j * block : (j + 1) * block, :] for j in range(chunks)], axis=1
        )
        for k in range(replicas)
    ]
    x_rows = jnp.concatenate(gathered, axis=0)
    parts = []
    for c in range(slots // LANES):
        lane_step = (iota((16, LANES), 1) + c * LANES) // block
        row = jnp.zeros((16, LANES), F32)
        for k in range(replicas):
            if k * block // LANES == c:
                row = jnp.where(
                    lane_step == k, messages[k][chunks * block :, :].astype(F32), row
                )
        parts.append(row)
    local = jnp.concatenate(parts, axis=1) if len(parts) > 1 else parts[0]
    local_ref[...] = local[:8]
    product = lax.dot_general(
        down_ref[...].reshape(count * rank, width),
        x_rows,
        (((1,), (1,)), ((), ())),
        preferred_element_type=F32,
    )
    total = jnp.zeros((rank, slots), F32)
    for a in range(count):
        total += jnp.where(local[:1] == a, product[a * rank : (a + 1) * rank], 0.0)
    partial_ref[...] = total


def expand_kernel(replicas, block, partial_ref, local_ref, up_ref, *returns):
    count, rank, columns = up_ref.shape
    shrink = jnp.sum(partial_ref[...], axis=0).astype(BF16).astype(F32)
    local = local_ref[:1]
    spread = jnp.concatenate(
        [jnp.where(local == a, shrink, 0.0) for a in range(count)], axis=0
    ).astype(BF16)
    term = lax.dot_general(
        spread,
        up_ref[...].reshape(count * rank, columns),
        (((0,), (0,)), ((), ())),
        preferred_element_type=F32,
    )
    term = (adapter_output_scale * term).astype(BF16)
    for k in range(replicas):
        returns[k][...] = term[k * block : (k + 1) * block]


def attention_kernel(
    kv_heads, refill_ref, q_ref, fresh_ref, key_ref, value_ref, part_ref, weight_ref, flat_ref
):
    tokens, heads, depth = q_ref.shape
    positions = key_ref.shape[1]
    group = heads // kv_heads
    scale = depth ** (-0.5)
    base = pl.program_id(0) * tokens
    q_flat = q_ref[...].reshape(tokens * heads, depth)
    cross = lax.dot_general(
        q_flat, fresh_ref[...], (((1,), (1,)), ((), ())), preferred_element_type=F32
    )
    shape = cross.shape
    own = iota(shape, 1) == (iota(shape, 0) // group)
    fresh = jnp.sum(jnp.where(own, cross, 0.0), axis=1, keepdims=True) * scale
    own_head = (iota((heads, positions), 1) % kv_heads) == (iota((heads, positions), 0) // group)
    eye = iota((heads, LANES), 1) == iota((heads, LANES), 0)
    for t in range(tokens):
        score = lax.dot_general(
            q_ref[t], key_ref[t], (((1,), (1,)), ((), ())), preferred_element_type=F32
        )
        keep = own_head & (refill_ref[base + t] != 1)
        score = jnp.where(keep, score * scale, mask_value)
        new = fresh[t * heads : (t + 1) * heads]
        top = jnp.maximum(jnp.max(score, axis=1, keepdims=True), new)
        weight = jnp.exp(score - top)
        new = jnp.exp(new - top)
        inverse = 1.0 / (jnp.sum(weight, axis=1, keepdims=True) + new)
        new = (new * inverse).astype(BF16).astype(F32)
        weight_ref[t : t + 1, :] = jnp.sum(jnp.where(eye, new, 0.0), axis=0, keepdims=True)
        flat_ref[t * heads : (t + 1) * heads, :] = jnp.dot(
            (weight * inverse).astype(BF16), value_ref[t], preferred_element_type=F32
        )
    for h in range(heads):
        part_ref[:, h * depth : (h + 1) * depth] = flat_ref[pl.ds(h, tokens, stride=heads), :]


def finish_kernel(replicas, kv_heads, heads, *refs):
    terms = refs[:replicas]
    order_ref, base_ref, part_ref, weight_ref, incoming_ref, attended_ref = refs[replicas:]
    depth = incoming_ref.shape[1] // kv_heads
    back = jnp.concatenate([term[...] for term in terms], axis=0)
    term = jnp.dot(order_ref[...], back, preferred_element_type=F32)
    incoming = (base_ref[...] + term).astype(BF16)
    incoming_ref[...] = incoming
    wide = incoming.astype(F32)
    for h in range(heads):
        k = h // (heads // kv_heads)
        at = slice(h * depth, (h + 1) * depth)
        attended_ref[:, at] = (
            part_ref[:, at] + weight_ref[:, h : h + 1] * wide[:, k * depth : (k + 1) * depth]
        ).astype(BF16)


def params(mib):
    return pltpu.CompilerParams(vmem_limit_bytes=mib * 2**20)


def cost(flops, size):
    return pl.CostEstimate(flops=flops, bytes_accessed=size, transcendentals=0)


def body(
    mesh_shape,
    normed_hidden_rows,
    queries,
    incoming_key,
    stored_key_cache,
    stored_value_cache,
    value_weight,
    adapter_down_weight,
    adapter_up_weight,
    token_adapter_index,
    adapter_holder_replica,
    refill,
):
    replicas = mesh_shape["replica"]
    rows, width = normed_hidden_rows.shape
    count, rank, slice_width = adapter_down_weight.shape
    columns = value_weight.shape[1]
    heads, depth = queries.shape[1:]
    kv_heads = incoming_key.shape[1]
    cache = stored_key_cache.shape[1]
    block = 16
    while block * replicas < rows:
        block *= 2
    slots = replicas * block
    message_rows = slice_width // LANES * block + 16
    pieces = 4

    routed = pl.pallas_call(
        functools.partial(route_kernel, replicas, block),
        out_shape=[jax.ShapeDtypeStruct((message_rows, LANES), BF16)] * replicas
        + [jax.ShapeDtypeStruct((rows, slots), BF16)],
        in_specs=[VMEM, VMEM, ANY],
        out_specs=[VMEM] * (replicas + 1),
        scratch_shapes=[
            pltpu.VMEM((rows, slice_width), BF16),
            pltpu.SemaphoreType.DMA((pieces,)),
        ],
        compiler_params=params(16),
        name="route",
    )(token_adapter_index.reshape(1, rows), adapter_holder_replica.reshape(1, -1), normed_hidden_rows)
    messages, order = routed[:replicas], routed[replicas]
    arrived = [messages[0]] + [None] * (replicas - 1)
    for k in range(replicas - 1, 0, -1):
        arrived[k] = lax.ppermute(messages[k], "replica", partner_pairs(replicas, k))

    tokens = 16
    part, new_weight = pl.pallas_call(
        functools.partial(attention_kernel, kv_heads),
        out_shape=[
            jax.ShapeDtypeStruct((rows, heads * depth), F32),
            jax.ShapeDtypeStruct((rows, LANES), F32),
        ],
        grid=(rows // tokens,),
        in_specs=[
            pl.BlockSpec(memory_space=pltpu.SMEM),
            pl.BlockSpec((tokens, heads, depth), lambda i: (i, 0, 0)),
            pl.BlockSpec((tokens * kv_heads, depth), lambda i: (i, 0)),
            pl.BlockSpec((tokens, cache * kv_heads, depth), lambda i: (i, 0, 0)),
            pl.BlockSpec((tokens, cache * kv_heads, depth), lambda i: (i, 0, 0)),
        ],
        out_specs=[
            pl.BlockSpec((tokens, heads * depth), lambda i: (i, 0)),
            pl.BlockSpec((tokens, LANES), lambda i: (i, 0)),
        ],
        scratch_shapes=[pltpu.VMEM((tokens * heads, depth), F32)],
        compiler_params=params(24),
        cost_estimate=cost(4 * rows * heads * cache * kv_heads * depth, 10 * 2**20),
        name="attend_cache",
    )(
        refill,
        queries,
        incoming_key.reshape(rows * kv_heads, depth),
        stored_key_cache.reshape(rows, cache * kv_heads, depth),
        stored_value_cache.reshape(rows, cache * kv_heads, depth),
    )
    base = jnp.dot(normed_hidden_rows, value_weight, preferred_element_type=F32)

    partial_shrink, local = pl.pallas_call(
        functools.partial(shrink_kernel, replicas, block),
        out_shape=[
            jax.ShapeDtypeStruct((rank, slots), F32),
            jax.ShapeDtypeStruct((8, slots), F32),
        ],
        in_specs=[VMEM] * (replicas + 1),
        out_specs=[VMEM] * 2,
        compiler_params=params(16),
        name="shrink",
    )(*arrived, adapter_down_weight)
    gathered = lax.all_gather(partial_shrink, "tensor", axis=0)
    returns = pl.pallas_call(
        functools.partial(expand_kernel, replicas, block),
        out_shape=[jax.ShapeDtypeStruct((block, columns), BF16)] * replicas,
        in_specs=[VMEM] * 3,
        out_specs=[VMEM] * replicas,
        compiler_params=params(16),
        name="expand",
    )(gathered, local, adapter_up_weight)
    terms = [returns[0]] + [
        lax.ppermute(returns[k], "replica", return_pairs(replicas, k)) for k in range(1, replicas)
    ]
    incoming_value, attended = pl.pallas_call(
        functools.partial(finish_kernel, replicas, kv_heads, heads),
        out_shape=[
            jax.ShapeDtypeStruct((rows, columns), BF16),
            jax.ShapeDtypeStruct((rows, heads * depth), BF16),
        ],
        in_specs=[VMEM] * (replicas + 4),
        out_specs=[VMEM] * 2,
        compiler_params=params(16),
        name="finish",
    )(*terms, order, base, part, new_weight)
    return (incoming_value, attended)


def solution(mesh):
    return jax.shard_map(
        functools.partial(body, dict(mesh.shape)),
        mesh=mesh,
        in_specs=(
            P(("groups", "replica"), None),
            P(("groups", "replica"), "tensor", None),
            P(("groups", "replica"), "tensor", None),
            P(("groups", "replica"), None, "tensor", None),
            P(("groups", "replica"), None, "tensor", None),
            P(None, "tensor"),
            P("replica", None, "tensor"),
            P("replica", None, "tensor"),
            P(("groups", "replica")),
            P("groups"),
            P(("groups", "replica")),
        ),
        out_specs=(P(("groups", "replica"), "tensor"), P(("groups", "replica"), "tensor")),
        check_vma=False,
    )
```

```python
import functools

import jax
import jax.numpy as jnp
from jax import lax
from jax.experimental import pallas as pl
from jax.experimental.pallas import tpu as pltpu
from jax.sharding import PartitionSpec as P

adapter_output_scale = 0.5
mask_value = -1e30
LANES = 128
VMEM = pl.BlockSpec(memory_space=pltpu.VMEM)
HBM = pl.BlockSpec(memory_space=pltpu.HBM)
F32 = jnp.float32
BF16 = jnp.bfloat16


def iota(shape, dimension):
    return lax.broadcasted_iota(jnp.int32, shape, dimension)


def to_column(row):
    size = row.shape[1]
    eye = iota((size, size), 0) == iota((size, size), 1)
    return jnp.sum(jnp.where(eye, row, 0.0), axis=1, keepdims=True)


def partner_pairs(replicas, step):
    if replicas & (replicas - 1) == 0:
        return [(r, r ^ step) for r in range(replicas)]
    return [(r, (r + step) % replicas) for r in range(replicas)]


def return_pairs(replicas, step):
    return [(b, a) for a, b in partner_pairs(replicas, step)]


def route_kernel(replicas, block, tokens_hbm, holder_hbm, x_ref, *refs):
    messages, order_ref = refs[:replicas], refs[replicas]
    tokens_ref, holder_ref, x_buf, sems, small_sems = refs[replicas + 1 :]
    rows, width = x_buf.shape
    pieces = sems.shape[0]
    small = [
        pltpu.make_async_copy(tokens_hbm, tokens_ref, small_sems.at[0]),
        pltpu.make_async_copy(holder_hbm, holder_ref, small_sems.at[1]),
    ]
    for copy in small:
        copy.start()
    piece = width // pieces
    first = lax.axis_index("tensor") * width
    copies = [
        pltpu.make_async_copy(
            x_ref.at[:, pl.ds(pl.multiple_of(first + i * piece, LANES), piece)],
            x_buf.at[:, pl.ds(i * piece, piece)],
            sems.at[i],
        )
        for i in range(pieces)
    ]
    for copy in copies:
        copy.start()
    for copy in small:
        copy.wait()
    me = lax.axis_index("replica")
    adapters = holder_ref.shape[1]
    holder_row = holder_ref[...].astype(F32)
    holder_col = to_column(holder_row)
    earlier = (holder_col == holder_row) & (
        iota((adapters, adapters), 1) < iota((adapters, adapters), 0)
    )
    rank_col = jnp.sum(jnp.where(earlier, 1.0, 0.0), axis=1, keepdims=True)
    uses = tokens_ref[...] == iota((adapters, rows), 0)
    owner_row = jnp.sum(jnp.where(uses, holder_col, 0.0), axis=0, keepdims=True)
    local_row = jnp.sum(jnp.where(uses, rank_col, 0.0), axis=0, keepdims=True)
    owner_col = to_column(owner_row)
    before = (owner_col == owner_row) & (iota((rows, rows), 0) < iota((rows, rows), 1))
    place_row = jnp.sum(jnp.where(before, 1.0, 0.0), axis=0, keepdims=True)
    owner_int = owner_row.astype(jnp.int32)
    if replicas & (replicas - 1) == 0:
        step_row = owner_int ^ me
    else:
        step_row = owner_int - me
        step_row = jnp.where(step_row < 0, step_row + replicas, step_row)
    target_row = step_row * block + place_row.astype(jnp.int32)
    target_col = to_column(target_row.astype(F32)).astype(jnp.int32)
    local_col = to_column(local_row)
    slots = replicas * block
    select = (target_row == iota((slots, rows), 0)).astype(F32).astype(BF16)
    restore = (target_col == iota((rows, slots), 1)).astype(F32)
    order_ref[...] = restore.astype(BF16)
    local_by_slot = jnp.sum(restore * local_col, axis=0, keepdims=True)
    for k in range(replicas):
        lane = k * block // LANES * LANES
        tail = jnp.broadcast_to(local_by_slot[:, lane : lane + LANES], (16, LANES))
        messages[k][width // LANES * block :, :] = tail.astype(BF16)
    for i, copy in enumerate(copies):
        copy.wait()
        moved = jnp.dot(
            select, x_buf[:, i * piece : (i + 1) * piece], preferred_element_type=F32
        ).astype(BF16)
        for k in range(replicas):
            for j in range(piece // LANES):
                at = (i * (piece // LANES) + j) * block
                messages[k][at : at + block, :] = moved[
                    k * block : (k + 1) * block, j * LANES : (j + 1) * LANES
                ]


def shrink_kernel(replicas, block, *refs):
    messages, down_ref, partial_ref, local_ref = refs[:replicas], *refs[replicas:]
    count, rank, width = down_ref.shape
    slots = replicas * block
    chunks = width // LANES
    gathered = [
        jnp.concatenate(
            [messages[k][j * block : (j + 1) * block, :] for j in range(chunks)], axis=1
        )
        for k in range(replicas)
    ]
    x_rows = jnp.concatenate(gathered, axis=0)
    parts = []
    for c in range(slots // LANES):
        lane_step = (iota((16, LANES), 1) + c * LANES) // block
        row = jnp.zeros((16, LANES), F32)
        for k in range(replicas):
            if k * block // LANES == c:
                row = jnp.where(
                    lane_step == k, messages[k][chunks * block :, :].astype(F32), row
                )
        parts.append(row)
    local = jnp.concatenate(parts, axis=1) if len(parts) > 1 else parts[0]
    local_ref[...] = local[:8]
    product = lax.dot_general(
        down_ref[...].reshape(count * rank, width),
        x_rows,
        (((1,), (1,)), ((), ())),
        preferred_element_type=F32,
    )
    total = jnp.zeros((rank, slots), F32)
    for a in range(count):
        total += jnp.where(local[:1] == a, product[a * rank : (a + 1) * rank], 0.0)
    partial_ref[...] = total


def expand_kernel(replicas, block, partial_ref, local_ref, up_ref, *returns):
    count, rank, columns = up_ref.shape
    shrink = jnp.sum(partial_ref[...], axis=0).astype(BF16).astype(F32)
    local = local_ref[:1]
    spread = jnp.concatenate(
        [jnp.where(local == a, shrink, 0.0) for a in range(count)], axis=0
    ).astype(BF16)
    term = lax.dot_general(
        spread,
        up_ref[...].reshape(count * rank, columns),
        (((0,), (0,)), ((), ())),
        preferred_element_type=F32,
    )
    term = (adapter_output_scale * term).astype(BF16)
    for k in range(replicas):
        returns[k][...] = term[k * block : (k + 1) * block]


def middle_kernel(
    kv_heads,
    refill_hbm,
    fresh_hbm,
    q_hbm,
    key_hbm,
    value_hbm,
    x_hbm,
    w_hbm,
    part_ref,
    weight_ref,
    base_ref,
    refill_ref,
    fresh_ref,
    q_ref,
    key_ref,
    value_ref,
    x_ref,
    w_ref,
    flat_ref,
    sems,
    small_sems,
):
    rows, heads, depth = q_ref.shape
    positions = key_ref.shape[1]
    width = w_ref.shape[0]
    pieces = sems.shape[0]
    tokens = rows // pieces
    piece = width // pieces
    group = heads // kv_heads
    scale = depth ** (-0.5)
    small = [
        pltpu.make_async_copy(refill_hbm, refill_ref, small_sems.at[0]),
        pltpu.make_async_copy(fresh_hbm, fresh_ref, small_sems.at[1]),
    ]
    for copy in small:
        copy.start()
    copies = []
    for i in range(pieces):
        some, columns = pl.ds(i * tokens, tokens), pl.ds(i * piece, piece)
        copies.append(
            [
                pltpu.make_async_copy(q_hbm.at[some], q_ref.at[some], sems.at[i, 0]),
                pltpu.make_async_copy(key_hbm.at[some], key_ref.at[some], sems.at[i, 1]),
                pltpu.make_async_copy(value_hbm.at[some], value_ref.at[some], sems.at[i, 2]),
                pltpu.make_async_copy(x_hbm.at[:, columns], x_ref.at[:, columns], sems.at[i, 3]),
                pltpu.make_async_copy(w_hbm.at[columns], w_ref.at[columns], sems.at[i, 4]),
            ]
        )
        for copy in copies[i]:
            copy.start()
    for copy in small:
        copy.wait()
    n = tokens * heads
    own_fresh = iota((n, tokens * kv_heads), 1) == (iota((n, tokens * kv_heads), 0) // group)
    own_head = (iota((n, positions), 1) % kv_heads) == ((iota((n, positions), 0) // group) % kv_heads)
    eye = iota((n, LANES), 1) == (iota((n, LANES), 0) % heads)
    refilled = refill_ref[...].astype(F32)
    for i in range(pieces):
        first = i * tokens
        for copy in copies[i]:
            copy.wait()
        cross = lax.dot_general(
            q_ref[first : first + tokens].reshape(n, depth),
            fresh_ref[first * kv_heads : (first + tokens) * kv_heads, :],
            (((1,), (1,)), ((), ())),
            preferred_element_type=F32,
        )
        fresh = jnp.sum(jnp.where(own_fresh, cross, 0.0), axis=1, keepdims=True) * scale
        mine = iota((n, rows), 1) == (first + iota((n, rows), 0) // heads)
        blocked = jnp.sum(jnp.where(mine, refilled, 0.0), axis=1, keepdims=True)
        score = lax.dot_general(
            q_ref[first : first + tokens],
            key_ref[first : first + tokens],
            (((2,), (2,)), ((0,), (0,))),
            preferred_element_type=F32,
        ).reshape(n, positions)
        keep = own_head & (blocked != 1.0)
        score = jnp.where(keep, score * scale, mask_value)
        top = jnp.maximum(jnp.max(score, axis=1, keepdims=True), fresh)
        weight = jnp.exp(score - top)
        new = jnp.exp(fresh - top)
        inverse = 1.0 / (jnp.sum(weight, axis=1, keepdims=True) + new)
        new = (new * inverse).astype(BF16).astype(F32)
        weight_ref[first : first + tokens, :] = jnp.sum(
            jnp.where(eye, new, 0.0).reshape(tokens, heads, LANES), axis=1
        )
        flat_ref[...] = lax.dot_general(
            (weight * inverse).astype(BF16).reshape(tokens, heads, positions),
            value_ref[first : first + tokens],
            (((2,), (1,)), ((0,), (0,))),
            preferred_element_type=F32,
        ).reshape(n, depth)
        for h in range(heads):
            part_ref[first : first + tokens, h * depth : (h + 1) * depth] = flat_ref[
                pl.ds(h, tokens, stride=heads), :
            ]
        product = jnp.dot(
            x_ref[:, i * piece : (i + 1) * piece],
            w_ref[i * piece : (i + 1) * piece, :],
            preferred_element_type=F32,
        )
        base_ref[...] = product if i == 0 else base_ref[...] + product


def finish_kernel(replicas, kv_heads, heads, *refs):
    terms = refs[:replicas]
    order_ref, base_ref, part_ref, weight_ref, incoming_ref, attended_ref = refs[replicas:]
    depth = incoming_ref.shape[1] // kv_heads
    back = jnp.concatenate([term[...] for term in terms], axis=0)
    term = jnp.dot(order_ref[...], back, preferred_element_type=F32)
    incoming = (base_ref[...] + term).astype(BF16)
    incoming_ref[...] = incoming
    wide = incoming.astype(F32)
    for h in range(heads):
        k = h // (heads // kv_heads)
        at = slice(h * depth, (h + 1) * depth)
        attended_ref[:, at] = (
            part_ref[:, at] + weight_ref[:, h : h + 1] * wide[:, k * depth : (k + 1) * depth]
        ).astype(BF16)


def in_hbm(*arrays):
    return [pltpu.with_memory_space_constraint(array, pltpu.HBM) for array in arrays]


def params(mib):
    return pltpu.CompilerParams(vmem_limit_bytes=mib * 2**20)


def cost(flops, size):
    return pl.CostEstimate(flops=flops, bytes_accessed=size, transcendentals=0)


def body(
    mesh_shape,
    normed_hidden_rows,
    queries,
    incoming_key,
    stored_key_cache,
    stored_value_cache,
    value_weight,
    adapter_down_weight,
    adapter_up_weight,
    token_adapter_index,
    adapter_holder_replica,
    refill,
):
    replicas = mesh_shape["replica"]
    rows, width = normed_hidden_rows.shape
    count, rank, slice_width = adapter_down_weight.shape
    columns = value_weight.shape[1]
    heads, depth = queries.shape[1:]
    kv_heads = incoming_key.shape[1]
    adapters = adapter_holder_replica.shape[0]
    cache = stored_key_cache.shape[1]
    block = 16
    while block * replicas < rows:
        block *= 2
    slots = replicas * block
    message_rows = slice_width // LANES * block + 16
    pieces = 4

    routed = pl.pallas_call(
        functools.partial(route_kernel, replicas, block),
        out_shape=[jax.ShapeDtypeStruct((message_rows, LANES), BF16)] * replicas
        + [jax.ShapeDtypeStruct((rows, slots), BF16)],
        in_specs=[HBM] * 3,
        out_specs=[VMEM] * (replicas + 1),
        scratch_shapes=[
            pltpu.VMEM((1, rows), jnp.int32),
            pltpu.VMEM((1, adapters), jnp.int32),
            pltpu.VMEM((rows, slice_width), BF16),
            pltpu.SemaphoreType.DMA((pieces,)),
            pltpu.SemaphoreType.DMA((2,)),
        ],
        compiler_params=params(16),
        name="route",
    )(
        *in_hbm(
            token_adapter_index.reshape(1, rows),
            adapter_holder_replica.reshape(1, adapters),
            normed_hidden_rows,
        )
    )
    messages, order = routed[:replicas], routed[replicas]
    arrived = [messages[0]] + [None] * (replicas - 1)
    for k in range(replicas - 1, 0, -1):
        arrived[k] = lax.ppermute(messages[k], "replica", partner_pairs(replicas, k))

    positions = cache * kv_heads
    parts = max(1, rows // 32)
    part, new_weight, base = pl.pallas_call(
        functools.partial(middle_kernel, kv_heads),
        out_shape=[
            jax.ShapeDtypeStruct((rows, heads * depth), F32),
            jax.ShapeDtypeStruct((rows, LANES), F32),
            jax.ShapeDtypeStruct((rows, columns), F32),
        ],
        in_specs=[HBM] * 7,
        out_specs=[VMEM] * 3,
        scratch_shapes=[
            pltpu.VMEM((1, rows), jnp.int32),
            pltpu.VMEM((rows * kv_heads, depth), BF16),
            pltpu.VMEM((rows, heads, depth), BF16),
            pltpu.VMEM((rows, positions, depth), BF16),
            pltpu.VMEM((rows, positions, depth), BF16),
            pltpu.VMEM((rows, width), BF16),
            pltpu.VMEM((width, columns), BF16),
            pltpu.VMEM((rows // parts * heads, depth), F32),
            pltpu.SemaphoreType.DMA((parts, 5)),
            pltpu.SemaphoreType.DMA((2,)),
        ],
        compiler_params=params(32),
        cost_estimate=cost(
            4 * rows * heads * positions * depth + 2 * rows * width * columns, 15 * 2**20
        ),
        name="middle",
    )(
        *in_hbm(
            refill.reshape(1, rows),
            incoming_key.reshape(rows * kv_heads, depth),
            queries,
            stored_key_cache.reshape(rows, positions, depth),
            stored_value_cache.reshape(rows, positions, depth),
            normed_hidden_rows,
            value_weight,
        )
    )
    part, *arrived = lax.optimization_barrier((part, *arrived))

    partial_shrink, local = pl.pallas_call(
        functools.partial(shrink_kernel, replicas, block),
        out_shape=[
            jax.ShapeDtypeStruct((rank, slots), F32),
            jax.ShapeDtypeStruct((8, slots), F32),
        ],
        in_specs=[VMEM] * (replicas + 1),
        out_specs=[VMEM] * 2,
        compiler_params=params(16),
        name="shrink",
    )(*arrived, adapter_down_weight)
    gathered = lax.all_gather(partial_shrink, "tensor", axis=0)
    returns = pl.pallas_call(
        functools.partial(expand_kernel, replicas, block),
        out_shape=[jax.ShapeDtypeStruct((block, columns), BF16)] * replicas,
        in_specs=[VMEM] * 3,
        out_specs=[VMEM] * replicas,
        compiler_params=params(16),
        name="expand",
    )(gathered, local, adapter_up_weight)
    terms = [returns[0]] + [
        lax.ppermute(returns[k], "replica", return_pairs(replicas, k)) for k in range(1, replicas)
    ]
    incoming_value, attended = pl.pallas_call(
        functools.partial(finish_kernel, replicas, kv_heads, heads),
        out_shape=[
            jax.ShapeDtypeStruct((rows, columns), BF16),
            jax.ShapeDtypeStruct((rows, heads * depth), BF16),
        ],
        in_specs=[VMEM] * (replicas + 4),
        out_specs=[VMEM] * 2,
        compiler_params=params(16),
        name="finish",
    )(*terms, order, base, part, new_weight)
    return (incoming_value, attended)


def solution(mesh):
    return jax.shard_map(
        functools.partial(body, dict(mesh.shape)),
        mesh=mesh,
        in_specs=(
            P(("groups", "replica"), None),
            P(("groups", "replica"), "tensor", None),
            P(("groups", "replica"), "tensor", None),
            P(("groups", "replica"), None, "tensor", None),
            P(("groups", "replica"), None, "tensor", None),
            P(None, "tensor"),
            P("replica", None, "tensor"),
            P("replica", None, "tensor"),
            P(("groups", "replica")),
            P("groups"),
            P(("groups", "replica")),
        ),
        out_specs=(P(("groups", "replica"), "tensor"), P(("groups", "replica"), "tensor")),
        check_vma=False,
    )
```

```python
import functools

import jax
import jax.numpy as jnp
from jax import lax
from jax.experimental import pallas as pl
from jax.experimental.pallas import tpu as pltpu
from jax.sharding import PartitionSpec as P

adapter_output_scale = 0.5
mask_value = -1e30
ahead = 2
together = 2
LANES = 128
VMEM = pl.BlockSpec(memory_space=pltpu.VMEM)
HBM = pl.BlockSpec(memory_space=pltpu.HBM)
F32 = jnp.float32
BF16 = jnp.bfloat16


def iota(shape, dimension):
    return lax.broadcasted_iota(jnp.int32, shape, dimension)


def to_column(row):
    size = row.shape[1]
    eye = iota((size, size), 0) == iota((size, size), 1)
    return jnp.sum(jnp.where(eye, row, 0.0), axis=1, keepdims=True)


def partner_pairs(replicas, step):
    if replicas & (replicas - 1) == 0:
        return [(r, r ^ step) for r in range(replicas)]
    return [(r, (r + step) % replicas) for r in range(replicas)]


def return_pairs(replicas, step):
    return [(b, a) for a, b in partner_pairs(replicas, step)]


def route_kernel(replicas, block, tokens_hbm, holder_hbm, x_ref, *refs):
    messages, order_ref = refs[:replicas], refs[replicas]
    tokens_ref, holder_ref, x_buf, sems, small_sems = refs[replicas + 1 :]
    rows, width = x_buf.shape
    pieces = sems.shape[0]
    small = [
        pltpu.make_async_copy(tokens_hbm, tokens_ref, small_sems.at[0]),
        pltpu.make_async_copy(holder_hbm, holder_ref, small_sems.at[1]),
    ]
    for copy in small:
        copy.start()
    piece = width // pieces
    first = lax.axis_index("tensor") * width
    copies = [
        pltpu.make_async_copy(
            x_ref.at[:, pl.ds(pl.multiple_of(first + i * piece, LANES), piece)],
            x_buf.at[:, pl.ds(i * piece, piece)],
            sems.at[i],
        )
        for i in range(pieces)
    ]
    for copy in copies:
        copy.start()
    for copy in small:
        copy.wait()
    me = lax.axis_index("replica")
    adapters = holder_ref.shape[1]
    holder_row = holder_ref[...].astype(F32)
    holder_col = to_column(holder_row)
    earlier = (holder_col == holder_row) & (
        iota((adapters, adapters), 1) < iota((adapters, adapters), 0)
    )
    rank_col = jnp.sum(jnp.where(earlier, 1.0, 0.0), axis=1, keepdims=True)
    uses = tokens_ref[...] == iota((adapters, rows), 0)
    owner_row = jnp.sum(jnp.where(uses, holder_col, 0.0), axis=0, keepdims=True)
    local_row = jnp.sum(jnp.where(uses, rank_col, 0.0), axis=0, keepdims=True)
    owner_col = to_column(owner_row)
    before = (owner_col == owner_row) & (iota((rows, rows), 0) < iota((rows, rows), 1))
    place_row = jnp.sum(jnp.where(before, 1.0, 0.0), axis=0, keepdims=True)
    owner_int = owner_row.astype(jnp.int32)
    if replicas & (replicas - 1) == 0:
        step_row = owner_int ^ me
    else:
        step_row = owner_int - me
        step_row = jnp.where(step_row < 0, step_row + replicas, step_row)
    target_row = step_row * block + place_row.astype(jnp.int32)
    target_col = to_column(target_row.astype(F32)).astype(jnp.int32)
    local_col = to_column(local_row)
    slots = replicas * block
    select = (target_row == iota((slots, rows), 0)).astype(F32).astype(BF16)
    restore = (target_col == iota((rows, slots), 1)).astype(F32)
    order_ref[...] = restore.astype(BF16)
    local_by_slot = jnp.sum(restore * local_col, axis=0, keepdims=True)
    for k in range(replicas):
        lane = k * block // LANES * LANES
        tail = jnp.broadcast_to(local_by_slot[:, lane : lane + LANES], (16, LANES))
        messages[k][width // LANES * block :, :] = tail.astype(BF16)
    for i, copy in enumerate(copies):
        copy.wait()
        moved = jnp.dot(
            select, x_buf[:, i * piece : (i + 1) * piece], preferred_element_type=F32
        ).astype(BF16)
        for k in range(replicas):
            for j in range(piece // LANES):
                at = (i * (piece // LANES) + j) * block
                messages[k][at : at + block, :] = moved[
                    k * block : (k + 1) * block, j * LANES : (j + 1) * LANES
                ]


def shrink_kernel(replicas, block, order_sent, *refs):
    down_ref, partial_ref, local_ref = refs[replicas:]
    messages = [None] * replicas
    for k, ref in zip(order_sent, refs):
        messages[k] = ref
    count, rank, width = down_ref.shape
    slots = replicas * block
    chunks = width // LANES
    gathered = [
        jnp.concatenate(
            [messages[k][j * block : (j + 1) * block, :] for j in range(chunks)], axis=1
        )
        for k in range(replicas)
    ]
    x_rows = jnp.concatenate(gathered, axis=0)
    parts = []
    for c in range(slots // LANES):
        lane_step = (iota((16, LANES), 1) + c * LANES) // block
        row = jnp.zeros((16, LANES), F32)
        for k in range(replicas):
            if k * block // LANES == c:
                row = jnp.where(
                    lane_step == k, messages[k][chunks * block :, :].astype(F32), row
                )
        parts.append(row)
    local = jnp.concatenate(parts, axis=1) if len(parts) > 1 else parts[0]
    local_ref[...] = local[:8]
    product = lax.dot_general(
        down_ref[...].reshape(count * rank, width),
        x_rows,
        (((1,), (1,)), ((), ())),
        preferred_element_type=F32,
    )
    total = jnp.zeros((rank, slots), F32)
    for a in range(count):
        total += jnp.where(local[:1] == a, product[a * rank : (a + 1) * rank], 0.0)
    partial_ref[...] = total


def expand_kernel(shards, replicas, block, *refs):
    partials, returns = refs[:shards], refs[shards + 2 :]
    local_ref, up_ref = refs[shards : shards + 2]
    count, rank, columns = up_ref.shape
    shrink = partials[0][...]
    for partial in partials[1:]:
        shrink += partial[...]
    shrink = shrink.astype(BF16).astype(F32)
    local = local_ref[:1]
    spread = jnp.concatenate(
        [jnp.where(local == a, shrink, 0.0) for a in range(count)], axis=0
    ).astype(BF16)
    term = lax.dot_general(
        spread,
        up_ref[...].reshape(count * rank, columns),
        (((0,), (0,)), ((), ())),
        preferred_element_type=F32,
    )
    term = (adapter_output_scale * term).astype(BF16)
    for k in range(replicas):
        returns[k][...] = term[k * block : (k + 1) * block]


def middle_kernel(
    kv_heads,
    refill_hbm,
    fresh_hbm,
    q_hbm,
    key_hbm,
    value_hbm,
    x_hbm,
    w_hbm,
    part_ref,
    weight_ref,
    base_ref,
    refill_ref,
    fresh_ref,
    q_ref,
    key_ref,
    value_ref,
    x_ref,
    w_ref,
    flat_ref,
    sems,
    small_sems,
):
    rows, heads, depth = q_ref.shape
    positions = key_ref.shape[1]
    width = w_ref.shape[0]
    pieces = sems.shape[0]
    tokens = rows // pieces
    piece = width // pieces
    group = heads // kv_heads
    scale = depth ** (-0.5)
    small = [
        pltpu.make_async_copy(refill_hbm, refill_ref, small_sems.at[0]),
        pltpu.make_async_copy(fresh_hbm, fresh_ref, small_sems.at[1]),
    ]
    for copy in small:
        copy.start()
    stages = []
    for i in range(pieces):
        some = pl.ds(i * tokens, tokens)
        stages.append(
            [
                pltpu.make_async_copy(q_hbm.at[some], q_ref.at[some], sems.at[i, 0]),
                pltpu.make_async_copy(key_hbm.at[some], key_ref.at[some], sems.at[i, 1]),
                pltpu.make_async_copy(value_hbm.at[some], value_ref.at[some], sems.at[i, 2]),
            ]
        )
    for i in range(pieces):
        some = pl.ds(i * piece, piece)
        stages.append(
            [
                pltpu.make_async_copy(x_hbm.at[:, some], x_ref.at[:, some], sems.at[i, 3]),
                pltpu.make_async_copy(w_hbm.at[some], w_ref.at[some], sems.at[i, 4]),
            ]
        )

    def start(stage):
        for copy in stages[stage] if stage < len(stages) else []:
            copy.start()

    def wait(stage):
        for copy in stages[stage]:
            copy.wait()

    for i in range(ahead):
        start(i)
    for copy in small:
        copy.wait()
    n = tokens * heads
    own_fresh = iota((n, tokens * kv_heads), 1) == (iota((n, tokens * kv_heads), 0) // group)
    wide = together * positions
    row, lane = iota((n, wide), 0), iota((n, wide), 1)
    own_head = (lane % kv_heads == row // group % kv_heads) & (
        lane // positions == row // heads % together
    )
    eye = iota((n, LANES), 1) == (iota((n, LANES), 0) % heads)
    refilled = refill_ref[...].astype(F32)
    for i in range(pieces):
        first = i * tokens
        wait(i)
        start(i + ahead)
        cross = lax.dot_general(
            q_ref[first : first + tokens].reshape(n, depth),
            fresh_ref[first * kv_heads : (first + tokens) * kv_heads, :],
            (((1,), (1,)), ((), ())),
            preferred_element_type=F32,
        )
        fresh = jnp.sum(jnp.where(own_fresh, cross, 0.0), axis=1, keepdims=True) * scale
        mine = iota((n, rows), 1) == (first + iota((n, rows), 0) // heads)
        blocked = jnp.sum(jnp.where(mine, refilled, 0.0), axis=1, keepdims=True)
        score = lax.dot_general(
            q_ref[first : first + tokens].reshape(tokens // together, together * heads, depth),
            key_ref[first : first + tokens].reshape(tokens // together, wide, depth),
            (((2,), (2,)), ((0,), (0,))),
            preferred_element_type=F32,
        ).reshape(n, wide)
        keep = own_head & (blocked != 1.0)
        score = jnp.where(keep, score * scale, mask_value)
        top = jnp.maximum(jnp.max(score, axis=1, keepdims=True), fresh)
        weight = jnp.exp(score - top)
        new = jnp.exp(fresh - top)
        inverse = 1.0 / (jnp.sum(weight, axis=1, keepdims=True) + new)
        new = (new * inverse).astype(BF16).astype(F32)
        weight_ref[first : first + tokens, :] = jnp.sum(
            jnp.where(eye, new, 0.0).reshape(tokens, heads, LANES), axis=1
        )
        flat_ref[...] = lax.dot_general(
            (weight * inverse).astype(BF16).reshape(tokens // together, together * heads, wide),
            value_ref[first : first + tokens].reshape(tokens // together, wide, depth),
            (((2,), (1,)), ((0,), (0,))),
            preferred_element_type=F32,
        ).reshape(n, depth)
        for h in range(heads):
            part_ref[first : first + tokens, h * depth : (h + 1) * depth] = flat_ref[
                pl.ds(h, tokens, stride=heads), :
            ]
    for i in range(pieces):
        wait(pieces + i)
        start(pieces + i + ahead)
        product = jnp.dot(
            x_ref[:, i * piece : (i + 1) * piece],
            w_ref[i * piece : (i + 1) * piece, :],
            preferred_element_type=F32,
        )
        base_ref[...] = product if i == 0 else base_ref[...] + product


def finish_kernel(replicas, kv_heads, heads, order_back, *refs):
    terms = [None] * replicas
    for k, ref in zip(order_back, refs):
        terms[k] = ref
    order_ref, base_ref, part_ref, weight_ref, incoming_ref, attended_ref = refs[replicas:]
    depth = incoming_ref.shape[1] // kv_heads
    back = jnp.concatenate([term[...] for term in terms], axis=0)
    term = jnp.dot(order_ref[...], back, preferred_element_type=F32)
    incoming = (base_ref[...] + term).astype(BF16)
    incoming_ref[...] = incoming
    wide = incoming.astype(F32)
    for h in range(heads):
        k = h // (heads // kv_heads)
        at = slice(h * depth, (h + 1) * depth)
        attended_ref[:, at] = (
            part_ref[:, at] + weight_ref[:, h : h + 1] * wide[:, k * depth : (k + 1) * depth]
        ).astype(BF16)


def in_hbm(*arrays):
    return [pltpu.with_memory_space_constraint(array, pltpu.HBM) for array in arrays]


def params(mib):
    return pltpu.CompilerParams(vmem_limit_bytes=mib * 2**20)


def cost(flops, size):
    return pl.CostEstimate(flops=flops, bytes_accessed=size, transcendentals=0)


def body(
    mesh_shape,
    normed_hidden_rows,
    queries,
    incoming_key,
    stored_key_cache,
    stored_value_cache,
    value_weight,
    adapter_down_weight,
    adapter_up_weight,
    token_adapter_index,
    adapter_holder_replica,
    refill,
):
    replicas = mesh_shape["replica"]
    rows, width = normed_hidden_rows.shape
    count, rank, slice_width = adapter_down_weight.shape
    columns = value_weight.shape[1]
    heads, depth = queries.shape[1:]
    kv_heads = incoming_key.shape[1]
    adapters = adapter_holder_replica.shape[0]
    cache = stored_key_cache.shape[1]
    block = 16
    while block * replicas < rows:
        block *= 2
    slots = replicas * block
    message_rows = slice_width // LANES * block + 16
    pieces = 4

    routed = pl.pallas_call(
        functools.partial(route_kernel, replicas, block),
        out_shape=[jax.ShapeDtypeStruct((message_rows, LANES), BF16)] * replicas
        + [jax.ShapeDtypeStruct((rows, slots), BF16)],
        in_specs=[HBM] * 3,
        out_specs=[VMEM] * (replicas + 1),
        scratch_shapes=[
            pltpu.VMEM((1, rows), jnp.int32),
            pltpu.VMEM((1, adapters), jnp.int32),
            pltpu.VMEM((rows, slice_width), BF16),
            pltpu.SemaphoreType.DMA((pieces,)),
            pltpu.SemaphoreType.DMA((2,)),
        ],
        compiler_params=params(16),
        name="route",
    )(
        *in_hbm(
            token_adapter_index.reshape(1, rows),
            adapter_holder_replica.reshape(1, adapters),
            normed_hidden_rows,
        )
    )
    messages, order = routed[:replicas], routed[replicas]
    arrived = [messages[0]] + [None] * (replicas - 1)
    order_sent = list(range(replicas - 1, 0, -1))
    for k in order_sent:
        arrived[k] = lax.ppermute(messages[k], "replica", partner_pairs(replicas, k))

    positions = cache * kv_heads
    parts = max(1, rows // 64)
    part, new_weight, base = pl.pallas_call(
        functools.partial(middle_kernel, kv_heads),
        out_shape=[
            jax.ShapeDtypeStruct((rows, heads * depth), F32),
            jax.ShapeDtypeStruct((rows, LANES), F32),
            jax.ShapeDtypeStruct((rows, columns), F32),
        ],
        in_specs=[HBM] * 7,
        out_specs=[VMEM] * 3,
        scratch_shapes=[
            pltpu.VMEM((1, rows), jnp.int32),
            pltpu.VMEM((rows * kv_heads, depth), BF16),
            pltpu.VMEM((rows, heads, depth), BF16),
            pltpu.VMEM((rows, positions, depth), BF16),
            pltpu.VMEM((rows, positions, depth), BF16),
            pltpu.VMEM((rows, width), BF16),
            pltpu.VMEM((width, columns), BF16),
            pltpu.VMEM((rows // parts * heads, depth), F32),
            pltpu.SemaphoreType.DMA((parts, 5)),
            pltpu.SemaphoreType.DMA((2,)),
        ],
        compiler_params=params(32),
        cost_estimate=cost(
            4 * rows * heads * positions * depth + 2 * rows * width * columns, 15 * 2**20
        ),
        name="middle",
    )(
        *in_hbm(
            refill.reshape(1, rows),
            incoming_key.reshape(rows * kv_heads, depth),
            queries,
            stored_key_cache.reshape(rows, positions, depth),
            stored_value_cache.reshape(rows, positions, depth),
            normed_hidden_rows,
            value_weight,
        )
    )
    part, *moved = lax.optimization_barrier((part, *[arrived[k] for k in order_sent]))
    for k, message in zip(order_sent, moved):
        arrived[k] = message

    partial_shrink, local = pl.pallas_call(
        functools.partial(shrink_kernel, replicas, block, order_sent + [0]),
        out_shape=[
            jax.ShapeDtypeStruct((rank, slots), F32),
            jax.ShapeDtypeStruct((8, slots), F32),
        ],
        in_specs=[VMEM] * (replicas + 1),
        out_specs=[VMEM] * 2,
        compiler_params=params(16),
        name="shrink",
    )(*[arrived[k] for k in order_sent + [0]], adapter_down_weight)
    shards = mesh_shape["tensor"]
    partials = [partial_shrink] + [
        lax.ppermute(partial_shrink, "tensor", partner_pairs(shards, k)) for k in range(1, shards)
    ]
    returns = pl.pallas_call(
        functools.partial(expand_kernel, shards, replicas, block),
        out_shape=[jax.ShapeDtypeStruct((block, columns), BF16)] * replicas,
        in_specs=[VMEM] * (shards + 2),
        out_specs=[VMEM] * replicas,
        compiler_params=params(16),
        name="expand",
    )(*partials, local, adapter_up_weight)
    terms = [returns[0]] + [
        lax.ppermute(returns[k], "replica", return_pairs(replicas, k)) for k in range(1, replicas)
    ]
    order_back = list(range(2, replicas)) + list(range(min(replicas, 2)))[::-1]
    incoming_value, attended = pl.pallas_call(
        functools.partial(finish_kernel, replicas, kv_heads, heads, order_back),
        out_shape=[
            jax.ShapeDtypeStruct((rows, columns), BF16),
            jax.ShapeDtypeStruct((rows, heads * depth), BF16),
        ],
        in_specs=[VMEM] * (replicas + 4),
        out_specs=[VMEM] * 2,
        compiler_params=params(16),
        name="finish",
    )(*[terms[k] for k in order_back], order, base, part, new_weight)
    return (incoming_value, attended)


def solution(mesh):
    return jax.shard_map(
        functools.partial(body, dict(mesh.shape)),
        mesh=mesh,
        in_specs=(
            P(("groups", "replica"), None),
            P(("groups", "replica"), "tensor", None),
            P(("groups", "replica"), "tensor", None),
            P(("groups", "replica"), None, "tensor", None),
            P(("groups", "replica"), None, "tensor", None),
            P(None, "tensor"),
            P("replica", None, "tensor"),
            P("replica", None, "tensor"),
            P(("groups", "replica")),
            P("groups"),
            P(("groups", "replica")),
        ),
        out_specs=(P(("groups", "replica"), "tensor"), P(("groups", "replica"), "tensor")),
        check_vma=False,
    )
```

```python
import functools

import jax
import jax.numpy as jnp
from jax import lax
from jax.experimental import pallas as pl
from jax.experimental.pallas import tpu as pltpu
from jax.sharding import PartitionSpec as P

adapter_output_scale = 0.5
mask_value = -1e30
ahead = 2
together = 2
LANES = 128
VMEM = pl.BlockSpec(memory_space=pltpu.VMEM)
HBM = pl.BlockSpec(memory_space=pltpu.HBM)
F32 = jnp.float32
BF16 = jnp.bfloat16


def iota(shape, dimension):
    return lax.broadcasted_iota(jnp.int32, shape, dimension)


def to_column(row):
    size = row.shape[1]
    eye = iota((size, size), 0) == iota((size, size), 1)
    return jnp.sum(jnp.where(eye, row, 0.0), axis=1, keepdims=True)


def partner_pairs(replicas, step):
    if replicas & (replicas - 1) == 0:
        return [(r, r ^ step) for r in range(replicas)]
    return [(r, (r + step) % replicas) for r in range(replicas)]


def return_pairs(replicas, step):
    return [(b, a) for a, b in partner_pairs(replicas, step)]


def route_kernel(replicas, block, tokens_hbm, holder_hbm, x_ref, *refs):
    messages, target_ref = refs[:replicas], refs[replicas]
    tokens_ref, holder_ref, x_buf, sems, small_sems = refs[replicas + 1 :]
    rows, width = x_buf.shape
    pieces = sems.shape[0]
    small = [
        pltpu.make_async_copy(tokens_hbm, tokens_ref, small_sems.at[0]),
        pltpu.make_async_copy(holder_hbm, holder_ref, small_sems.at[1]),
    ]
    for copy in small:
        copy.start()
    piece = width // pieces
    first = lax.axis_index("tensor") * width
    copies = [
        pltpu.make_async_copy(
            x_ref.at[:, pl.ds(pl.multiple_of(first + i * piece, LANES), piece)],
            x_buf.at[:, pl.ds(i * piece, piece)],
            sems.at[i],
        )
        for i in range(pieces)
    ]
    for copy in copies:
        copy.start()
    for copy in small:
        copy.wait()
    me = lax.axis_index("replica")
    adapters = holder_ref.shape[1]
    holder_row = holder_ref[...].astype(F32)
    holder_col = to_column(holder_row)
    earlier = (holder_col == holder_row) & (
        iota((adapters, adapters), 1) < iota((adapters, adapters), 0)
    )
    rank_col = jnp.sum(jnp.where(earlier, 1.0, 0.0), axis=1, keepdims=True)
    uses = tokens_ref[...] == iota((adapters, rows), 0)
    owner_row = jnp.sum(jnp.where(uses, holder_col, 0.0), axis=0, keepdims=True).astype(jnp.int32)
    local_row = jnp.sum(jnp.where(uses, rank_col, 0.0), axis=0, keepdims=True)
    owned = (owner_row == iota((max(replicas, 16), rows), 0)).astype(F32)
    before = (iota((rows, rows), 0) < iota((rows, rows), 1)).astype(F32).astype(BF16)
    count = jnp.dot(owned.astype(BF16), before, preferred_element_type=F32)
    place_row = jnp.sum(owned * count, axis=0, keepdims=True).astype(jnp.int32)
    if replicas & (replicas - 1) == 0:
        step_row = owner_row ^ me
    else:
        step_row = owner_row - me
        step_row = jnp.where(step_row < 0, step_row + replicas, step_row)
    target_row = step_row * block + place_row
    target_ref[...] = target_row
    slots = replicas * block
    select = (target_row == iota((slots, rows), 0)).astype(F32).astype(BF16)
    local_by_slot = lax.dot_general(
        jnp.broadcast_to(local_row, (16, rows)).astype(BF16),
        select,
        (((1,), (1,)), ((), ())),
        preferred_element_type=F32,
    ).astype(BF16)
    for k in range(replicas):
        lane = k * block // LANES * LANES
        messages[k][width // LANES * block :, :] = local_by_slot[:, lane : lane + LANES]
    for i, copy in enumerate(copies):
        copy.wait()
        moved = jnp.dot(
            select, x_buf[:, i * piece : (i + 1) * piece], preferred_element_type=F32
        ).astype(BF16)
        for k in range(replicas):
            for j in range(piece // LANES):
                at = (i * (piece // LANES) + j) * block
                messages[k][at : at + block, :] = moved[
                    k * block : (k + 1) * block, j * LANES : (j + 1) * LANES
                ]


def shrink_kernel(replicas, block, order_sent, *refs):
    down_ref, partial_ref, sent_ref, local_ref = refs[replicas:]
    messages = [None] * replicas
    for k, ref in zip(order_sent, refs):
        messages[k] = ref
    count, rank, width = down_ref.shape
    slots = replicas * block
    chunks = width // LANES
    gathered = [
        jnp.concatenate(
            [messages[k][j * block : (j + 1) * block, :] for j in range(chunks)], axis=1
        )
        for k in range(replicas)
    ]
    x_rows = jnp.concatenate(gathered, axis=0)
    parts = []
    for c in range(slots // LANES):
        lane_step = (iota((16, LANES), 1) + c * LANES) // block
        row = jnp.zeros((16, LANES), F32)
        for k in range(replicas):
            if k * block // LANES == c:
                row = jnp.where(
                    lane_step == k, messages[k][chunks * block :, :].astype(F32), row
                )
        parts.append(row)
    local = jnp.concatenate(parts, axis=1) if len(parts) > 1 else parts[0]
    local_ref[...] = local[:8]
    product = lax.dot_general(
        down_ref[...].reshape(count * rank, width),
        x_rows,
        (((1,), (1,)), ((), ())),
        preferred_element_type=F32,
    )
    total = jnp.zeros((rank, slots), F32)
    for a in range(count):
        total += jnp.where(local[:1] == a, product[a * rank : (a + 1) * rank], 0.0)
    partial_ref[...] = total
    sent_ref[...] = total.astype(BF16)


def expand_kernel(shards, replicas, block, *refs):
    partials, returns = refs[:shards], refs[shards + 2 :]
    local_ref, up_ref = refs[shards : shards + 2]
    count, rank, columns = up_ref.shape
    shrink = partials[0][...]
    for partial in partials[1:]:
        shrink += partial[...].astype(F32)
    shrink = shrink.astype(BF16).astype(F32)
    local = local_ref[:1]
    spread = jnp.concatenate(
        [jnp.where(local == a, shrink, 0.0) for a in range(count)], axis=0
    ).astype(BF16)
    term = lax.dot_general(
        spread,
        up_ref[...].reshape(count * rank, columns),
        (((0,), (0,)), ((), ())),
        preferred_element_type=F32,
    )
    term = (adapter_output_scale * term).astype(BF16)
    for k in range(replicas):
        returns[k][...] = term[k * block : (k + 1) * block]


def middle_kernel(
    kv_heads,
    target_ref,
    refill_hbm,
    fresh_hbm,
    q_hbm,
    key_hbm,
    value_hbm,
    x_hbm,
    w_hbm,
    part_ref,
    weight_ref,
    base_ref,
    order_ref,
    refill_ref,
    fresh_ref,
    q_ref,
    key_ref,
    value_ref,
    x_ref,
    w_ref,
    flat_ref,
    sems,
    small_sems,
):
    rows, heads, depth = q_ref.shape
    positions = key_ref.shape[1]
    width = w_ref.shape[0]
    pieces = sems.shape[0]
    tokens = rows // pieces
    piece = width // pieces
    group = heads // kv_heads
    scale = depth ** (-0.5)
    small = [
        pltpu.make_async_copy(refill_hbm, refill_ref, small_sems.at[0]),
        pltpu.make_async_copy(fresh_hbm, fresh_ref, small_sems.at[1]),
    ]
    for copy in small:
        copy.start()
    stages = []
    for i in range(pieces):
        some = pl.ds(i * tokens, tokens)
        stages.append(
            [
                pltpu.make_async_copy(q_hbm.at[some], q_ref.at[some], sems.at[i, 0]),
                pltpu.make_async_copy(key_hbm.at[some], key_ref.at[some], sems.at[i, 1]),
                pltpu.make_async_copy(value_hbm.at[some], value_ref.at[some], sems.at[i, 2]),
            ]
        )
    for i in range(pieces):
        some = pl.ds(i * piece, piece)
        stages.append(
            [
                pltpu.make_async_copy(x_hbm.at[:, some], x_ref.at[:, some], sems.at[i, 3]),
                pltpu.make_async_copy(w_hbm.at[some], w_ref.at[some], sems.at[i, 4]),
            ]
        )

    def start(stage):
        for copy in stages[stage] if stage < len(stages) else []:
            copy.start()

    def wait(stage):
        for copy in stages[stage]:
            copy.wait()

    for i in range(ahead):
        start(i)
    for copy in small:
        copy.wait()
    target_col = to_column(target_ref[...].astype(F32)).astype(jnp.int32)
    order_ref[...] = (target_col == iota(order_ref.shape, 1)).astype(F32).astype(BF16)
    n = tokens * heads
    own_fresh = iota((n, tokens * kv_heads), 1) == (iota((n, tokens * kv_heads), 0) // group)
    wide = together * positions
    row, lane = iota((n, wide), 0), iota((n, wide), 1)
    own_head = (lane % kv_heads == row // group % kv_heads) & (
        lane // positions == row // heads % together
    )
    eye = iota((n, LANES), 1) == (iota((n, LANES), 0) % heads)
    refilled = refill_ref[...].astype(F32)
    for i in range(pieces):
        first = i * tokens
        wait(i)
        start(i + ahead)
        cross = lax.dot_general(
            q_ref[first : first + tokens].reshape(n, depth),
            fresh_ref[first * kv_heads : (first + tokens) * kv_heads, :],
            (((1,), (1,)), ((), ())),
            preferred_element_type=F32,
        )
        fresh = jnp.sum(jnp.where(own_fresh, cross, 0.0), axis=1, keepdims=True) * scale
        mine = iota((n, rows), 1) == (first + iota((n, rows), 0) // heads)
        blocked = jnp.sum(jnp.where(mine, refilled, 0.0), axis=1, keepdims=True)
        score = lax.dot_general(
            q_ref[first : first + tokens].reshape(tokens // together, together * heads, depth),
            key_ref[first : first + tokens].reshape(tokens // together, wide, depth),
            (((2,), (2,)), ((0,), (0,))),
            preferred_element_type=F32,
        ).reshape(n, wide)
        keep = own_head & (blocked != 1.0)
        score = jnp.where(keep, score * scale, mask_value)
        top = jnp.maximum(jnp.max(score, axis=1, keepdims=True), fresh)
        weight = jnp.exp(score - top)
        new = jnp.exp(fresh - top)
        inverse = 1.0 / (jnp.sum(weight, axis=1, keepdims=True) + new)
        new = (new * inverse).astype(BF16).astype(F32)
        weight_ref[first : first + tokens, :] = jnp.sum(
            jnp.where(eye, new, 0.0).reshape(tokens, heads, LANES), axis=1
        )
        flat_ref[...] = lax.dot_general(
            (weight * inverse).astype(BF16).reshape(tokens // together, together * heads, wide),
            value_ref[first : first + tokens].reshape(tokens // together, wide, depth),
            (((2,), (1,)), ((0,), (0,))),
            preferred_element_type=F32,
        ).reshape(n, depth)
        for h in range(heads):
            part_ref[first : first + tokens, h * depth : (h + 1) * depth] = flat_ref[
                pl.ds(h, tokens, stride=heads), :
            ]
    for i in range(pieces):
        wait(pieces + i)
        start(pieces + i + ahead)
        product = jnp.dot(
            x_ref[:, i * piece : (i + 1) * piece],
            w_ref[i * piece : (i + 1) * piece, :],
            preferred_element_type=F32,
        )
        base_ref[...] = product if i == 0 else base_ref[...] + product


def finish_kernel(replicas, kv_heads, heads, order_back, *refs):
    terms = [None] * replicas
    for k, ref in zip(order_back, refs):
        terms[k] = ref
    order_ref, base_ref, part_ref, weight_ref, incoming_ref, attended_ref = refs[replicas:]
    depth = incoming_ref.shape[1] // kv_heads
    back = jnp.concatenate([term[...] for term in terms], axis=0)
    term = jnp.dot(order_ref[...], back, preferred_element_type=F32)
    incoming = (base_ref[...] + term).astype(BF16)
    incoming_ref[...] = incoming
    wide = incoming.astype(F32)
    for h in range(heads):
        k = h // (heads // kv_heads)
        at = slice(h * depth, (h + 1) * depth)
        attended_ref[:, at] = (
            part_ref[:, at] + weight_ref[:, h : h + 1] * wide[:, k * depth : (k + 1) * depth]
        ).astype(BF16)


def in_hbm(*arrays):
    return [pltpu.with_memory_space_constraint(array, pltpu.HBM) for array in arrays]


def params(mib):
    return pltpu.CompilerParams(vmem_limit_bytes=mib * 2**20)


def cost(flops, size):
    return pl.CostEstimate(flops=flops, bytes_accessed=size, transcendentals=0)


def body(
    mesh_shape,
    normed_hidden_rows,
    queries,
    incoming_key,
    stored_key_cache,
    stored_value_cache,
    value_weight,
    adapter_down_weight,
    adapter_up_weight,
    token_adapter_index,
    adapter_holder_replica,
    refill,
):
    replicas = mesh_shape["replica"]
    rows, width = normed_hidden_rows.shape
    count, rank, slice_width = adapter_down_weight.shape
    columns = value_weight.shape[1]
    heads, depth = queries.shape[1:]
    kv_heads = incoming_key.shape[1]
    adapters = adapter_holder_replica.shape[0]
    cache = stored_key_cache.shape[1]
    block = 16
    while block * replicas < rows:
        block *= 2
    slots = replicas * block
    message_rows = slice_width // LANES * block + 16
    pieces = 1

    routed = pl.pallas_call(
        functools.partial(route_kernel, replicas, block),
        out_shape=[jax.ShapeDtypeStruct((message_rows, LANES), BF16)] * replicas
        + [jax.ShapeDtypeStruct((1, rows), jnp.int32)],
        in_specs=[HBM] * 3,
        out_specs=[VMEM] * (replicas + 1),
        scratch_shapes=[
            pltpu.VMEM((1, rows), jnp.int32),
            pltpu.VMEM((1, adapters), jnp.int32),
            pltpu.VMEM((rows, slice_width), BF16),
            pltpu.SemaphoreType.DMA((pieces,)),
            pltpu.SemaphoreType.DMA((2,)),
        ],
        compiler_params=params(16),
        name="route",
    )(
        *in_hbm(
            token_adapter_index.reshape(1, rows),
            adapter_holder_replica.reshape(1, adapters),
            normed_hidden_rows,
        )
    )
    messages, target = routed[:replicas], routed[replicas]
    arrived = [messages[0]] + [None] * (replicas - 1)
    order_sent = list(range(replicas - 1, 0, -1))
    for k in order_sent:
        arrived[k] = lax.ppermute(messages[k], "replica", partner_pairs(replicas, k))

    positions = cache * kv_heads
    parts = max(1, rows // 64)
    part, new_weight, base, order = pl.pallas_call(
        functools.partial(middle_kernel, kv_heads),
        out_shape=[
            jax.ShapeDtypeStruct((rows, heads * depth), F32),
            jax.ShapeDtypeStruct((rows, LANES), F32),
            jax.ShapeDtypeStruct((rows, columns), F32),
            jax.ShapeDtypeStruct((rows, slots), BF16),
        ],
        in_specs=[VMEM] + [HBM] * 7,
        out_specs=[VMEM] * 4,
        scratch_shapes=[
            pltpu.VMEM((1, rows), jnp.int32),
            pltpu.VMEM((rows * kv_heads, depth), BF16),
            pltpu.VMEM((rows, heads, depth), BF16),
            pltpu.VMEM((rows, positions, depth), BF16),
            pltpu.VMEM((rows, positions, depth), BF16),
            pltpu.VMEM((rows, width), BF16),
            pltpu.VMEM((width, columns), BF16),
            pltpu.VMEM((rows // parts * heads, depth), F32),
            pltpu.SemaphoreType.DMA((parts, 5)),
            pltpu.SemaphoreType.DMA((2,)),
        ],
        compiler_params=params(32),
        cost_estimate=cost(
            4 * rows * heads * positions * depth + 2 * rows * width * columns, 15 * 2**20
        ),
        name="middle",
    )(
        target,
        *in_hbm(
            refill.reshape(1, rows),
            incoming_key.reshape(rows * kv_heads, depth),
            queries,
            stored_key_cache.reshape(rows, positions, depth),
            stored_value_cache.reshape(rows, positions, depth),
            normed_hidden_rows,
            value_weight,
        )
    )
    part, *moved = lax.optimization_barrier((part, *[arrived[k] for k in order_sent]))
    for k, message in zip(order_sent, moved):
        arrived[k] = message

    partial_shrink, sent_shrink, local = pl.pallas_call(
        functools.partial(shrink_kernel, replicas, block, order_sent + [0]),
        out_shape=[
            jax.ShapeDtypeStruct((rank, slots), F32),
            jax.ShapeDtypeStruct((rank, slots), BF16),
            jax.ShapeDtypeStruct((8, slots), F32),
        ],
        in_specs=[VMEM] * (replicas + 1),
        out_specs=[VMEM] * 3,
        compiler_params=params(16),
        name="shrink",
    )(*[arrived[k] for k in order_sent + [0]], adapter_down_weight)
    shards = mesh_shape["tensor"]
    partials = [partial_shrink] + [
        lax.ppermute(sent_shrink, "tensor", partner_pairs(shards, k)) for k in range(1, shards)
    ]
    returns = pl.pallas_call(
        functools.partial(expand_kernel, shards, replicas, block),
        out_shape=[jax.ShapeDtypeStruct((block, columns), BF16)] * replicas,
        in_specs=[VMEM] * (shards + 2),
        out_specs=[VMEM] * replicas,
        compiler_params=params(16),
        name="expand",
    )(*partials, local, adapter_up_weight)
    terms = [returns[0]] + [
        lax.ppermute(returns[k], "replica", return_pairs(replicas, k)) for k in range(1, replicas)
    ]
    order_back = list(range(2, replicas)) + list(range(min(replicas, 2)))[::-1]
    incoming_value, attended = pl.pallas_call(
        functools.partial(finish_kernel, replicas, kv_heads, heads, order_back),
        out_shape=[
            jax.ShapeDtypeStruct((rows, columns), BF16),
            jax.ShapeDtypeStruct((rows, heads * depth), BF16),
        ],
        in_specs=[VMEM] * (replicas + 4),
        out_specs=[VMEM] * 2,
        compiler_params=params(16),
        name="finish",
    )(*[terms[k] for k in order_back], order, base, part, new_weight)
    return (incoming_value, attended)


def solution(mesh):
    return jax.shard_map(
        functools.partial(body, dict(mesh.shape)),
        mesh=mesh,
        in_specs=(
            P(("groups", "replica"), None),
            P(("groups", "replica"), "tensor", None),
            P(("groups", "replica"), "tensor", None),
            P(("groups", "replica"), None, "tensor", None),
            P(("groups", "replica"), None, "tensor", None),
            P(None, "tensor"),
            P("replica", None, "tensor"),
            P("replica", None, "tensor"),
            P(("groups", "replica")),
            P("groups"),
            P(("groups", "replica")),
        ),
        out_specs=(P(("groups", "replica"), "tensor"), P(("groups", "replica"), "tensor")),
        check_vma=False,
    )
```

```python
import functools

import jax
import jax.numpy as jnp
from jax import lax
from jax.experimental import pallas as pl
from jax.experimental.pallas import tpu as pltpu
from jax.sharding import PartitionSpec as P

adapter_output_scale = 0.5
mask_value = -1e30
ahead = 2
together = 2
LANES = 128
VMEM = pl.BlockSpec(memory_space=pltpu.VMEM)
HBM = pl.BlockSpec(memory_space=pltpu.HBM)
F32 = jnp.float32
BF16 = jnp.bfloat16


def iota(shape, dimension):
    return lax.broadcasted_iota(jnp.int32, shape, dimension)


def to_column(row):
    size = row.shape[1]
    eye = iota((size, size), 0) == iota((size, size), 1)
    return jnp.sum(jnp.where(eye, row, 0.0), axis=1, keepdims=True)


def partner_pairs(replicas, step):
    if replicas & (replicas - 1) == 0:
        return [(r, r ^ step) for r in range(replicas)]
    return [(r, (r + step) % replicas) for r in range(replicas)]


def return_pairs(replicas, step):
    return [(b, a) for a, b in partner_pairs(replicas, step)]


def route_kernel(replicas, block, tokens_hbm, holder_hbm, x_ref, *refs):
    messages, target_ref = refs[:replicas], refs[replicas]
    tokens_ref, holder_ref, x_buf, sems, small_sems = refs[replicas + 1 :]
    rows, width = x_buf.shape
    pieces = sems.shape[0]
    small = [
        pltpu.make_async_copy(tokens_hbm, tokens_ref, small_sems.at[0]),
        pltpu.make_async_copy(holder_hbm, holder_ref, small_sems.at[1]),
    ]
    for copy in small:
        copy.start()
    piece = width // pieces
    first = lax.axis_index("tensor") * width
    copies = [
        pltpu.make_async_copy(
            x_ref.at[:, pl.ds(pl.multiple_of(first + i * piece, LANES), piece)],
            x_buf.at[:, pl.ds(i * piece, piece)],
            sems.at[i],
        )
        for i in range(pieces)
    ]
    for copy in copies:
        copy.start()
    for copy in small:
        copy.wait()
    me = lax.axis_index("replica")
    adapters = holder_ref.shape[1]
    holder_row = holder_ref[...].astype(F32)
    holder_col = to_column(holder_row)
    earlier = (holder_col == holder_row) & (
        iota((adapters, adapters), 1) < iota((adapters, adapters), 0)
    )
    rank_col = jnp.sum(jnp.where(earlier, 1.0, 0.0), axis=1, keepdims=True)
    uses = tokens_ref[...] == iota((adapters, rows), 0)
    owner_row = jnp.sum(jnp.where(uses, holder_col, 0.0), axis=0, keepdims=True).astype(jnp.int32)
    local_row = jnp.sum(jnp.where(uses, rank_col, 0.0), axis=0, keepdims=True)
    owned = (owner_row == iota((max(replicas, 16), rows), 0)).astype(F32)
    before = (iota((rows, rows), 0) < iota((rows, rows), 1)).astype(F32).astype(BF16)
    count = jnp.dot(owned.astype(BF16), before, preferred_element_type=F32)
    place_row = jnp.sum(owned * count, axis=0, keepdims=True).astype(jnp.int32)
    if replicas & (replicas - 1) == 0:
        step_row = owner_row ^ me
    else:
        step_row = owner_row - me
        step_row = jnp.where(step_row < 0, step_row + replicas, step_row)
    target_row = step_row * block + place_row
    target_ref[...] = target_row
    slots = replicas * block
    select = (target_row == iota((slots, rows), 0)).astype(F32).astype(BF16)
    local_by_slot = lax.dot_general(
        jnp.broadcast_to(local_row, (16, rows)).astype(BF16),
        select,
        (((1,), (1,)), ((), ())),
        preferred_element_type=F32,
    ).astype(BF16)
    for k in range(replicas):
        lane = k * block // LANES * LANES
        messages[k][width // LANES * block :, :] = local_by_slot[:, lane : lane + LANES]
    for i, copy in enumerate(copies):
        copy.wait()
        moved = jnp.dot(
            select, x_buf[:, i * piece : (i + 1) * piece], preferred_element_type=F32
        ).astype(BF16)
        for k in range(replicas):
            for j in range(piece // LANES):
                at = (i * (piece // LANES) + j) * block
                messages[k][at : at + block, :] = moved[
                    k * block : (k + 1) * block, j * LANES : (j + 1) * LANES
                ]


def shrink_kernel(replicas, block, order_sent, *refs):
    down_ref, partial_ref, sent_ref, local_ref = refs[replicas:]
    messages = [None] * replicas
    for k, ref in zip(order_sent, refs):
        messages[k] = ref
    count, rank, width = down_ref.shape
    slots = replicas * block
    chunks = width // LANES
    gathered = [
        jnp.concatenate(
            [messages[k][j * block : (j + 1) * block, :] for j in range(chunks)], axis=1
        )
        for k in range(replicas)
    ]
    x_rows = jnp.concatenate(gathered, axis=0)
    parts = []
    for c in range(slots // LANES):
        lane_step = (iota((16, LANES), 1) + c * LANES) // block
        row = jnp.zeros((16, LANES), F32)
        for k in range(replicas):
            if k * block // LANES == c:
                row = jnp.where(
                    lane_step == k, messages[k][chunks * block :, :].astype(F32), row
                )
        parts.append(row)
    local = jnp.concatenate(parts, axis=1) if len(parts) > 1 else parts[0]
    local_ref[...] = local[:8]
    product = lax.dot_general(
        down_ref[...].reshape(count * rank, width),
        x_rows,
        (((1,), (1,)), ((), ())),
        preferred_element_type=F32,
    )
    total = jnp.zeros((rank, slots), F32)
    for a in range(count):
        total += jnp.where(local[:1] == a, product[a * rank : (a + 1) * rank], 0.0)
    partial_ref[...] = total
    sent_ref[...] = total.astype(BF16)


def expand_kernel(shards, replicas, block, *refs):
    partials, returns = refs[:shards], refs[shards + 2 :]
    local_ref, up_ref = refs[shards : shards + 2]
    count, rank, columns = up_ref.shape
    shrink = partials[0][...]
    for partial in partials[1:]:
        shrink += partial[...].astype(F32)
    shrink = shrink.astype(BF16).astype(F32)
    local = local_ref[:1]
    spread = jnp.concatenate(
        [jnp.where(local == a, shrink, 0.0) for a in range(count)], axis=0
    ).astype(BF16)
    term = lax.dot_general(
        spread,
        up_ref[...].reshape(count * rank, columns),
        (((0,), (0,)), ((), ())),
        preferred_element_type=F32,
    )
    term = (adapter_output_scale * term).astype(BF16)
    for k in range(replicas):
        returns[k][...] = term[k * block : (k + 1) * block]


def middle_kernel(
    kv_heads,
    target_ref,
    refill_hbm,
    fresh_hbm,
    q_hbm,
    key_hbm,
    value_hbm,
    x_hbm,
    w_hbm,
    part_ref,
    weight_ref,
    base_ref,
    order_ref,
    refill_ref,
    fresh_ref,
    q_ref,
    key_ref,
    value_ref,
    x_ref,
    w_ref,
    flat_ref,
    wide_ref,
    sems,
    small_sems,
):
    rows, heads, depth = q_ref.shape
    positions = key_ref.shape[1]
    width = w_ref.shape[0]
    pieces = sems.shape[0]
    tokens = rows // pieces
    piece = width // pieces
    group = heads // kv_heads
    scale = depth ** (-0.5)
    small = [
        pltpu.make_async_copy(refill_hbm, refill_ref, small_sems.at[0]),
        pltpu.make_async_copy(fresh_hbm, fresh_ref, small_sems.at[1]),
    ]
    for copy in small:
        copy.start()
    stages = []
    for i in range(pieces):
        some = pl.ds(i * tokens, tokens)
        stages.append(
            [
                pltpu.make_async_copy(q_hbm.at[some], q_ref.at[some], sems.at[i, 0]),
                pltpu.make_async_copy(key_hbm.at[some], key_ref.at[some], sems.at[i, 1]),
                pltpu.make_async_copy(value_hbm.at[some], value_ref.at[some], sems.at[i, 2]),
            ]
        )
    for i in range(pieces):
        some = pl.ds(i * piece, piece)
        stages.append(
            [
                pltpu.make_async_copy(x_hbm.at[:, some], x_ref.at[:, some], sems.at[i, 3]),
                pltpu.make_async_copy(w_hbm.at[some], w_ref.at[some], sems.at[i, 4]),
            ]
        )

    def start(stage):
        for copy in stages[stage] if stage < len(stages) else []:
            copy.start()

    def wait(stage):
        for copy in stages[stage]:
            copy.wait()

    for i in range(ahead):
        start(i)
    for copy in small:
        copy.wait()
    target_col = to_column(target_ref[...].astype(F32)).astype(jnp.int32)
    order_ref[...] = (target_col == iota(order_ref.shape, 1)).astype(F32).astype(BF16)
    n = tokens * heads
    own_fresh = iota((n, tokens * kv_heads), 1) == (iota((n, tokens * kv_heads), 0) // group)
    wide = together * positions
    row, lane = iota((n, wide), 0), iota((n, wide), 1)
    own_head = (lane % kv_heads == row // group % kv_heads) & (
        lane // positions == row // heads % together
    )
    refilled = refill_ref[...].astype(F32)
    for i in range(pieces):
        first = i * tokens
        wait(i)
        start(i + ahead)
        cross = lax.dot_general(
            q_ref[first : first + tokens].reshape(n, depth),
            fresh_ref[first * kv_heads : (first + tokens) * kv_heads, :],
            (((1,), (1,)), ((), ())),
            preferred_element_type=F32,
        )
        fresh = jnp.sum(jnp.where(own_fresh, cross, 0.0), axis=1, keepdims=True) * scale
        mine = iota((n, rows), 1) == (first + iota((n, rows), 0) // heads)
        blocked = jnp.sum(jnp.where(mine, refilled, 0.0), axis=1, keepdims=True)
        score = lax.dot_general(
            q_ref[first : first + tokens].reshape(tokens // together, together * heads, depth),
            key_ref[first : first + tokens].reshape(tokens // together, wide, depth),
            (((2,), (2,)), ((0,), (0,))),
            preferred_element_type=F32,
        ).reshape(n, wide)
        keep = own_head & (blocked != 1.0)
        score = jnp.where(keep, score * scale, mask_value)
        top = jnp.maximum(jnp.max(score, axis=1, keepdims=True), fresh)
        weight = jnp.exp(score - top)
        new = jnp.exp(fresh - top)
        inverse = 1.0 / (jnp.sum(weight, axis=1, keepdims=True) + new)
        new = (new * inverse).astype(BF16).astype(F32)
        wide_ref[...] = jnp.broadcast_to(new, (n, depth))
        flat_ref[...] = lax.dot_general(
            (weight * inverse).astype(BF16).reshape(tokens // together, together * heads, wide),
            value_ref[first : first + tokens].reshape(tokens // together, wide, depth),
            (((2,), (1,)), ((0,), (0,))),
            preferred_element_type=F32,
        ).reshape(n, depth)
        for h in range(heads):
            at = slice(h * depth, (h + 1) * depth)
            part_ref[first : first + tokens, at] = flat_ref[pl.ds(h, tokens, stride=heads), :]
            weight_ref[first : first + tokens, at] = wide_ref[pl.ds(h, tokens, stride=heads), :]
    for i in range(pieces):
        wait(pieces + i)
        start(pieces + i + ahead)
        product = jnp.dot(
            x_ref[:, i * piece : (i + 1) * piece],
            w_ref[i * piece : (i + 1) * piece, :],
            preferred_element_type=F32,
        )
        base_ref[...] = product if i == 0 else base_ref[...] + product


def finish_kernel(replicas, kv_heads, heads, order_back, *refs):
    terms = [None] * replicas
    for k, ref in zip(order_back, refs):
        terms[k] = ref
    order_ref, base_ref, part_ref, weight_ref = refs[replicas : replicas + 4]
    incoming_hbm, attended_hbm, incoming_ref, attended_ref, sems = refs[replicas + 4 :]
    rows, columns = incoming_ref.shape
    depth = columns // kv_heads
    pieces = sems.shape[0]
    piece = rows // pieces
    back = jnp.concatenate([term[...] for term in terms], axis=0)
    copies = []
    for i in range(pieces):
        some = slice(i * piece, (i + 1) * piece)
        term = jnp.dot(order_ref[some, :], back, preferred_element_type=F32)
        incoming = (base_ref[some, :] + term).astype(BF16)
        incoming_ref[some, :] = incoming
        wide = incoming.astype(F32)
        for h in range(heads):
            k = h // (heads // kv_heads)
            at = slice(h * depth, (h + 1) * depth)
            attended_ref[some, at] = (
                part_ref[some, at] + weight_ref[some, at] * wide[:, k * depth : (k + 1) * depth]
            ).astype(BF16)
        lines = pl.ds(i * piece, piece)
        for j, (source, result) in enumerate(
            [(incoming_ref, incoming_hbm), (attended_ref, attended_hbm)]
        ):
            copy = pltpu.make_async_copy(source.at[lines], result.at[lines], sems.at[i, j])
            copy.start()
            copies.append(copy)
    for copy in copies:
        copy.wait()


def in_hbm(*arrays):
    return [pltpu.with_memory_space_constraint(array, pltpu.HBM) for array in arrays]


def params(mib):
    return pltpu.CompilerParams(vmem_limit_bytes=mib * 2**20)


def cost(flops, size):
    return pl.CostEstimate(flops=flops, bytes_accessed=size, transcendentals=0)


def body(
    mesh_shape,
    normed_hidden_rows,
    queries,
    incoming_key,
    stored_key_cache,
    stored_value_cache,
    value_weight,
    adapter_down_weight,
    adapter_up_weight,
    token_adapter_index,
    adapter_holder_replica,
    refill,
):
    replicas = mesh_shape["replica"]
    rows, width = normed_hidden_rows.shape
    count, rank, slice_width = adapter_down_weight.shape
    columns = value_weight.shape[1]
    heads, depth = queries.shape[1:]
    kv_heads = incoming_key.shape[1]
    adapters = adapter_holder_replica.shape[0]
    cache = stored_key_cache.shape[1]
    block = 16
    while block * replicas < rows:
        block *= 2
    slots = replicas * block
    message_rows = slice_width // LANES * block + 16
    pieces = 1

    routed = pl.pallas_call(
        functools.partial(route_kernel, replicas, block),
        out_shape=[jax.ShapeDtypeStruct((message_rows, LANES), BF16)] * replicas
        + [jax.ShapeDtypeStruct((1, rows), jnp.int32)],
        in_specs=[HBM] * 3,
        out_specs=[VMEM] * (replicas + 1),
        scratch_shapes=[
            pltpu.VMEM((1, rows), jnp.int32),
            pltpu.VMEM((1, adapters), jnp.int32),
            pltpu.VMEM((rows, slice_width), BF16),
            pltpu.SemaphoreType.DMA((pieces,)),
            pltpu.SemaphoreType.DMA((2,)),
        ],
        compiler_params=params(16),
        name="route",
    )(
        *in_hbm(
            token_adapter_index.reshape(1, rows),
            adapter_holder_replica.reshape(1, adapters),
            normed_hidden_rows,
        )
    )
    messages, target = routed[:replicas], routed[replicas]
    arrived = [messages[0]] + [None] * (replicas - 1)
    order_sent = list(range(replicas - 1, 0, -1))
    for k in order_sent:
        arrived[k] = lax.ppermute(messages[k], "replica", partner_pairs(replicas, k))

    positions = cache * kv_heads
    parts = max(1, rows // 64)
    part, new_weight, base, order = pl.pallas_call(
        functools.partial(middle_kernel, kv_heads),
        out_shape=[
            jax.ShapeDtypeStruct((rows, heads * depth), F32),
            jax.ShapeDtypeStruct((rows, heads * depth), F32),
            jax.ShapeDtypeStruct((rows, columns), F32),
            jax.ShapeDtypeStruct((rows, slots), BF16),
        ],
        in_specs=[VMEM] + [HBM] * 7,
        out_specs=[VMEM] * 4,
        scratch_shapes=[
            pltpu.VMEM((1, rows), jnp.int32),
            pltpu.VMEM((rows * kv_heads, depth), BF16),
            pltpu.VMEM((rows, heads, depth), BF16),
            pltpu.VMEM((rows, positions, depth), BF16),
            pltpu.VMEM((rows, positions, depth), BF16),
            pltpu.VMEM((rows, width), BF16),
            pltpu.VMEM((width, columns), BF16),
            pltpu.VMEM((rows // parts * heads, depth), F32),
            pltpu.VMEM((rows // parts * heads, depth), F32),
            pltpu.SemaphoreType.DMA((parts, 5)),
            pltpu.SemaphoreType.DMA((2,)),
        ],
        compiler_params=params(32),
        cost_estimate=cost(
            4 * rows * heads * positions * depth + 2 * rows * width * columns, 15 * 2**20
        ),
        name="middle",
    )(
        target,
        *in_hbm(
            refill.reshape(1, rows),
            incoming_key.reshape(rows * kv_heads, depth),
            queries,
            stored_key_cache.reshape(rows, positions, depth),
            stored_value_cache.reshape(rows, positions, depth),
            normed_hidden_rows,
            value_weight,
        )
    )
    part, *moved = lax.optimization_barrier((part, *[arrived[k] for k in order_sent]))
    for k, message in zip(order_sent, moved):
        arrived[k] = message

    partial_shrink, sent_shrink, local = pl.pallas_call(
        functools.partial(shrink_kernel, replicas, block, order_sent + [0]),
        out_shape=[
            jax.ShapeDtypeStruct((rank, slots), F32),
            jax.ShapeDtypeStruct((rank, slots), BF16),
            jax.ShapeDtypeStruct((8, slots), F32),
        ],
        in_specs=[VMEM] * (replicas + 1),
        out_specs=[VMEM] * 3,
        compiler_params=params(16),
        name="shrink",
    )(*[arrived[k] for k in order_sent + [0]], adapter_down_weight)
    shards = mesh_shape["tensor"]
    partials = [partial_shrink] + [
        lax.ppermute(sent_shrink, "tensor", partner_pairs(shards, k)) for k in range(1, shards)
    ]
    returns = pl.pallas_call(
        functools.partial(expand_kernel, shards, replicas, block),
        out_shape=[jax.ShapeDtypeStruct((block, columns), BF16)] * replicas,
        in_specs=[VMEM] * (shards + 2),
        out_specs=[VMEM] * replicas,
        compiler_params=params(16),
        name="expand",
    )(*partials, local, adapter_up_weight)
    terms = [returns[0]] + [
        lax.ppermute(returns[k], "replica", return_pairs(replicas, k)) for k in range(1, replicas)
    ]
    out_pieces = 4
    order_back = list(range(2, replicas)) + list(range(min(replicas, 2)))[::-1]
    incoming_value, attended = pl.pallas_call(
        functools.partial(finish_kernel, replicas, kv_heads, heads, order_back),
        out_shape=[
            jax.ShapeDtypeStruct((rows, columns), BF16),
            jax.ShapeDtypeStruct((rows, heads * depth), BF16),
        ],
        in_specs=[VMEM] * (replicas + 4),
        out_specs=[HBM] * 2,
        scratch_shapes=[
            pltpu.VMEM((rows, columns), BF16),
            pltpu.VMEM((rows, heads * depth), BF16),
            pltpu.SemaphoreType.DMA((out_pieces, 2)),
        ],
        compiler_params=params(16),
        name="finish",
    )(*[terms[k] for k in order_back], order, base, part, new_weight)
    return (incoming_value, attended)


def solution(mesh):
    return jax.shard_map(
        functools.partial(body, dict(mesh.shape)),
        mesh=mesh,
        in_specs=(
            P(("groups", "replica"), None),
            P(("groups", "replica"), "tensor", None),
            P(("groups", "replica"), "tensor", None),
            P(("groups", "replica"), None, "tensor", None),
            P(("groups", "replica"), None, "tensor", None),
            P(None, "tensor"),
            P("replica", None, "tensor"),
            P("replica", None, "tensor"),
            P(("groups", "replica")),
            P("groups"),
            P(("groups", "replica")),
        ),
        out_specs=(P(("groups", "replica"), "tensor"), P(("groups", "replica"), "tensor")),
        check_vma=False,
    )
```
